128 devices in a mesh: dp: 16 (over x_hi, z, core), tensor: 8 (over y, x_lo).
Axes of the slice: x: 4 (x_hi: 2, x_lo: 2; x = x_hi * 2 + x_lo), y: 4, z: 4, core: 2. Of those that a mesh axis runs over, the one named last changes fastest.
Arguments:
- teacher_hidden: bfloat16 [8192, 7168], P('dp', 'tensor'), may hold values from -6 to 6
- teacher_down: bfloat16 [7168, 5120], P('tensor'), may hold values from -0.0625 to 0.0625
- student_in: bfloat16 [8192, 4096], P(('dp', 'tensor')), may hold values from -6 to 6
- student_weight: bfloat16 [4096, 4096], P('dp', 'tensor'), may hold values from -0.09375 to 0.09375
- projection: bfloat16 [5120, 4096], P('dp', 'tensor'), may hold values from -0.078125 to 0.078125
Outputs:
- grad_weight: float32 [4096, 4096], P('dp', 'tensor')
- grad_projection: float32 [5120, 4096], P('dp', 'tensor')
The draws below stay inside these ranges and needn't reach their ends.
All inputs are finite; a program needn't handle non-finite values.
Results may differ from the reference program's by a relative error of at most 0.003.
Values may be sent and summed in bfloat16 or wider, within the bound.
A program may use at most 128 MiB of HBM per device.

```python
import math
import jax
import jax.numpy as jnp

DT = 5120
FT = 7168
DS = 4096
TOKENS = 8192


def block_scale(rng, dims, pieces, least, high):
    factor_of, own = 1.0, jax.random.fold_in(rng, 6)
    for position, parts in pieces:
        draws = jnp.exp(jax.random.uniform(jax.random.fold_in(own, position), (parts,), jnp.float32, least / len(pieces), high / len(pieces)))
        factor_of = factor_of * jnp.repeat(draws, dims[position] // parts).reshape([-1 if axis == position else 1 for axis in range(len(dims))])
    return factor_of


def noise(key, dims, deviation, limit, cuts=(), dtype=jnp.bfloat16):
    array = jax.random.normal(key, dims, jnp.float32) * deviation
    if len(cuts) > 0:
        array = block_scale(key, dims, cuts, -0.22, 0.18) * array
    return jnp.clip(array, min=-limit, max=limit).astype(dtype)


def setup_inputs(seed: int = 0) -> dict:
    streams_of = jax.random.split(jax.random.key(seed), 6)
    return {
        "teacher_hidden": noise(streams_of[0], (TOKENS, FT), 1.0, 6.0, ((0, 16), (1, 8))),
        "teacher_down": noise(streams_of[1], (FT, DT), FT ** -0.5, 0.0625, ((0, 8),)),
        "student_in": noise(streams_of[2], (TOKENS, DS), 1.0, 6.0, ((0, 128),)),
        "student_weight": noise(streams_of[3], (DS, DS), DS ** -0.5, 0.09375, ((0, 16), (1, 8))),
        "projection": noise(streams_of[4], (DT, DS), DT ** -0.5, 0.078125, ((0, 16), (1, 8))),
    }


def reference(teacher_hidden, teacher_down, student_in, student_weight, projection):
    teacher_out = jnp.dot(teacher_hidden, teacher_down, preferred_element_type=jnp.float32).astype(jnp.bfloat16)
    student_out = jnp.dot(student_in, student_weight, preferred_element_type=jnp.float32)
    target = jnp.dot(teacher_out, projection, preferred_element_type=jnp.float32)
    residual = (student_out - target).astype(jnp.bfloat16)
    factor = 1.0 / math.sqrt(TOKENS)
    grad_weight = jnp.dot(student_in.T, residual, preferred_element_type=jnp.float32) * factor
    grad_projection = jnp.dot(teacher_out.T, residual, preferred_element_type=jnp.float32) * factor
    return (grad_weight, grad_projection)
```

```python
import functools
import math

import jax
import jax.numpy as jnp
from jax import lax
from jax.experimental import pallas as pl
from jax.experimental.pallas import tpu as pltpu
from jax.sharding import PartitionSpec as P

MESH = pl.DeviceIdType.MESH
BF16 = jnp.bfloat16
F32 = jnp.float32


class Place:
    def __init__(self):
        self.d = lax.axis_index("dp")
        self.t = lax.axis_index("tensor")
        self.core = lax.rem(self.d, 2)
        self.q = lax.div(self.d, 2)
        self.z = lax.rem(self.q, 4)
        self.xh = lax.div(self.q, 4)
        self.y = lax.div(self.t, 2)
        self.xl = lax.rem(self.t, 2)

    def dev(self, dy=0, dx=0, dz=0, dh=0, dc=0):
        d = self.dp(dz, dh, dc)
        return (d, self.tensor(dy, dx))

    def tensor(self, dy=0, dx=0):
        return lax.rem(self.y + dy + 4, 4) * 2 + lax.rem(self.xl + dx, 2)

    def chip(self, dz=0, dh=0):
        return lax.rem(self.xh + dh, 2) * 4 + lax.rem(self.z + dz + 4, 4)

    def dp(self, dz=0, dh=0, dc=0):
        return self.chip(dz, dh) * 2 + lax.rem(self.core + dc, 2)


class Copies:
    def __init__(self, send, recv, local):
        self.send, self.recv, self.local = send, recv, local
        self.n = 0
        self.m = 0
        self.sent = []
        self.kept = []

    def remote(self, src, dst, to):
        c = pltpu.make_async_remote_copy(
            src_ref=src,
            dst_ref=dst,
            send_sem=self.send.at[self.n],
            recv_sem=self.recv.at[self.n],
            device_id=to,
            device_id_type=MESH,
        )
        self.n += 1
        c.start()
        self.sent.append(c)
        return c

    def keep(self, src, dst):
        c = pltpu.make_async_copy(src, dst, self.local.at[self.m])
        self.m += 1
        c.start()
        self.kept.append(c)
        return c

    def drain(self):
        for c in self.kept:
            c.wait()
        for c in self.sent:
            c.wait_send()


def barrier(devices):
    sem = pltpu.get_barrier_semaphore()
    for dev in devices:
        pl.semaphore_signal(sem, inc=1, device_id=dev, device_id_type=MESH)
    pl.semaphore_wait(sem, len(devices))


def columns(index, width):
    return pl.ds(pl.multiple_of(index * width, 128), width)


def gather_tensor(cp, me, own, place, cut):
    first = {}
    first["x0"] = cp.remote(own(0), place(me.t, 0), me.dev(dx=1))
    for k in (1, 3, 2):
        first["y1", k] = cp.remote(own(1), place(me.t, 1), me.dev(dy=k))
    for k in (1, 3, 2):
        first["y0", k] = cp.remote(own(0), place(me.t, 0), me.dev(dy=k))
    first["x1"] = cp.remote(own(1), place(me.t, 1), me.dev(dx=1))
    second = {}

    def forward():
        first["x0"].wait_recv()
        tx = me.tensor(dx=1)
        for k in (1, 3, 2):
            second["y", k] = cp.remote(place(tx, 0), place(tx, 0), me.dev(dy=k))
        for k in (1, 3, 2):
            first["y1", k].wait_recv()
            ty = me.tensor(dy=-k)
            second["x", k] = cp.remote(place(ty, 1), place(ty, 1), me.dev(dx=1))

    def finish(done):
        for k in (1, 3, 2):
            first["y0", k].wait_recv()
            done(me.tensor(dy=-k))
        first["x1"].wait_recv()
        done(me.tensor(dx=1))
        for k in (1, 3, 2):
            second["y", k].wait_recv()
            second["x", k].wait_recv()
            done(me.tensor(dy=-k, dx=1))

    return forward, finish


def nothing(t):
    return None


def hidden_and_down(h, d, hh, dd, send, recv, local):
    me = Place()
    cp = Copies(send, recv, local)
    piece = me.z * 2 + me.core
    tensor_peers = [me.dev(dy=a, dx=b) for a in range(4) for b in range(2) if a or b]
    z_peers = [me.dev(dz=k) for k in (1, 3, 2)]
    barrier(tensor_peers + z_peers + [me.dev(dc=1)])

    rows = pl.ds(pl.multiple_of(piece * 112, 16), 112)
    cp.keep(d.at[rows, columns(me.t, 640)], dd.at[me.t, piece])
    handed = []
    for a, b in ((0, 1), (1, 0), (3, 0), (2, 0), (1, 1), (3, 1), (2, 1)):
        to = me.tensor(dy=a, dx=b)
        handed.append(
            cp.remote(d.at[rows, columns(to, 640)], dd.at[me.t, piece], me.dev(dy=a, dx=b))
        )
    cp.keep(h, hh.at[:, columns(me.t, 896)])

    part = (pl.ds(0, 320), pl.ds(320, 192))
    forward, finish = gather_tensor(
        cp,
        me,
        lambda p: h.at[part[p]],
        lambda t, p: hh.at[part[p], columns(t, 896)],
        part,
    )
    cp.kept[0].wait()
    cp.kept.pop(0)
    for c in handed:
        c.wait_recv()
    over_z = []
    for k in (1, 3, 2):
        over_z.append(cp.remote(dd.at[:, piece], dd.at[:, piece], me.dev(dz=k)))
    side = [cp.remote(dd.at[:, piece], dd.at[:, piece], me.dev(dc=1))]
    forward()
    for k, c in zip((1, 3, 2), over_z):
        c.wait_recv()
        theirs = lax.rem(me.z - k + 4, 4) * 2 + me.core
        side.append(cp.remote(dd.at[:, theirs], dd.at[:, theirs], me.dev(dc=1)))
    finish(nothing)
    for c in side:
        c.wait_recv()
    cp.drain()


def rows_and_weights(s, t, w, p, ss, tt, ww, pp, send, recv, local):
    me = Place()
    cp = Copies(send, recv, local)
    y_peers = [me.dev(dy=k) for k in (1, 3, 2)]
    z_peers = [me.dev(dz=k) for k in (1, 3, 2)]
    sibling = me.dev(dc=1)
    barrier(y_peers + z_peers + [sibling, me.dev(dx=1), me.dev(dh=1)])

    mine = columns(me.core, 256)
    other = columns(1 - me.core, 256)
    cp.keep(w.at[:, mine], ww.at[me.q, me.core])
    cp.keep(p.at[:, mine], pp.at[me.q, me.core])
    swap = [
        cp.remote(w.at[:, other], ww.at[me.q, me.core], sibling),
        cp.remote(p.at[:, other], pp.at[me.q, me.core], sibling),
    ]
    s_part = (pl.ds(0, 32), pl.ds(32, 32))
    t_part = (pl.ds(0, 336), pl.ds(336, 176))
    s_place = lambda b, q: ss.at[me.core, b, s_part[q]]
    t_place = lambda b, q: tt.at[me.core, t_part[q], columns(b, 640)]
    s_forward, s_finish = gather_tensor(cp, me, lambda q: s.at[s_part[q]], s_place, s_part)
    t_forward, t_finish = gather_tensor(cp, me, lambda q: t.at[t_part[q]], t_place, t_part)
    cp.keep(s, ss.at[me.core, me.t])
    cp.keep(t, tt.at[me.core, :, columns(me.t, 640)])

    side = [
        cp.remote(s, ss.at[me.core, me.t], sibling),
        cp.remote(t, tt.at[me.core, :, columns(me.t, 640)], sibling),
    ]
    for c in cp.kept[:2]:
        c.wait()
    del cp.kept[:2]
    for c in swap:
        c.wait_recv()
    over = []
    for ref in (ww, pp):
        over.append(cp.remote(ref.at[me.q], ref.at[me.q], me.dev(dh=1)))
    from_z = []
    for ref in (ww, pp):
        for k in (1, 3, 2):
            from_z.append(cp.remote(ref.at[me.q], ref.at[me.q], me.dev(dz=k)))
    s_forward()
    t_forward()
    far = me.chip(dh=1)
    for ref, c in zip((ww, pp), over):
        c.wait_recv()
        for k in (1, 3, 2):
            from_z.append(cp.remote(ref.at[far], ref.at[far], me.dev(dz=k)))

    def s_side(b):
        block = ss.at[me.core, b]
        side.append(cp.remote(block, block, sibling))

    def t_side(b):
        block = tt.at[me.core, :, columns(b, 640)]
        side.append(cp.remote(block, block, sibling))

    s_finish(s_side)
    t_finish(t_side)
    for c in from_z:
        c.wait_recv()
    for c in side:
        c.wait_recv()
    cp.drain()


def scatter_sums(factor, gw, gp, ow, op, rw, rp, tw, tp, send, recv, local):
    me = Place()
    cp = Copies(send, recv, local)
    offsets = [(a, b) for b in (0, 1) for a in (1, 3, 2, 0) if a or b]
    peers = [me.dev(dz=a, dh=b) for a, b in offsets]
    sibling = me.dev(dc=1)
    barrier(peers + [sibling])
    arrivals = []
    for slot, (a, b) in enumerate(offsets):
        q = me.chip(dz=a, dh=b)
        arrivals.append(cp.remote(gw.at[:, columns(q, 512)], rw.at[slot], me.dev(dz=a, dh=b)))
        arrivals.append(cp.remote(gp.at[:, columns(q, 640)], rp.at[slot], me.dev(dz=a, dh=b)))
    cp.keep(gw.at[:, columns(me.q, 512)], rw.at[7])
    cp.keep(gp.at[:, columns(me.q, 640)], rp.at[7])
    for c in cp.kept:
        c.wait()
    cp.kept.clear()
    for c in arrivals:
        c.wait_recv()

    def add(r, out, tiles):
        for i in range(tiles):
            block = slice(i * 128, i * 128 + 128)
            total = r[7, :, block].astype(F32)
            for slot in range(7):
                total += r[slot, :, block].astype(F32)
            out[block, :] = (total * factor).T

    add(rw, tw, 4)
    add(rp, tp, 5)
    last = []
    mine = columns(me.core, 256)
    for staged, out, rows in ((tw, ow, 256), (tp, op, 320)):
        theirs = pl.ds(pl.multiple_of((1 - me.core) * rows, 64), rows)
        ours = pl.ds(pl.multiple_of(me.core * rows, 64), rows)
        last.append(cp.remote(staged.at[theirs], out.at[:, mine], sibling))
        cp.keep(staged.at[ours], out.at[:, mine])
    for c in last:
        c.wait_recv()
    cp.drain()


ANY = pl.BlockSpec(memory_space=pl.ANY)
VMEM = pl.BlockSpec(memory_space=pltpu.VMEM)


def dma(n):
    return pltpu.SemaphoreType.DMA((n,))


def call(kernel, ident, outs, args, copies, kept, scratch=(), out_spec=ANY):
    return pl.pallas_call(
        kernel,
        out_shape=[jax.ShapeDtypeStruct(shape, dtype) for shape, dtype in outs],
        in_specs=[ANY] * len(args),
        out_specs=[out_spec] * len(outs),
        scratch_shapes=[*scratch, dma(copies), dma(copies), dma(kept)],
        compiler_params=pltpu.CompilerParams(
            collective_id=ident, has_side_effects=True, vmem_limit_bytes=48 * 2**20
        ),
    )(*args)


def dot(a, b, ca, cb):
    return lax.dot_general(a, b, (((ca,), (cb,)), ((), ())), preferred_element_type=F32)


def on_device(teacher_hidden, teacher_down, student_in, student_weight, projection):
    factor = 1.0 / math.sqrt(8192)
    hidden, down = call(
        hidden_and_down,
        1,
        [((512, 7168), BF16), ((8, 8, 112, 640), BF16)],
        (teacher_hidden, teacher_down),
        28,
        2,
    )
    block = dot(hidden, down.reshape(7168, 640), 1, 0).astype(BF16)
    rows, teacher, weight, proj = call(
        rows_and_weights,
        2,
        [((2, 8, 64, 4096), BF16), ((2, 512, 5120), BF16), ((8, 2, 256, 256), BF16), ((8, 2, 320, 256), BF16)],
        (student_in, block, student_weight, projection),
        60,
        4,
    )
    rows = rows.reshape(1024, 4096)
    teacher = teacher.reshape(1024, 5120)
    residual = (
        dot(rows, weight.reshape(4096, 256), 1, 0) - dot(teacher, proj.reshape(5120, 256), 1, 0)
    ).astype(BF16)
    grad_weight = dot(residual, rows, 0, 0).astype(BF16)
    grad_projection = dot(residual, teacher, 0, 0).astype(BF16)
    return call(
        functools.partial(scatter_sums, factor),
        3,
        [((256, 512), F32), ((320, 512), F32)],
        (grad_weight, grad_projection),
        16,
        4,
        (
            pltpu.VMEM((8, 256, 512), BF16),
            pltpu.VMEM((8, 256, 640), BF16),
            pltpu.VMEM((512, 256), F32),
            pltpu.VMEM((640, 256), F32),
        ),
        VMEM,
    )


def solution(mesh):
    in_specs = (
        P("dp", "tensor"),
        P("tensor", None),
        P(("dp", "tensor"), None),
        P("dp", "tensor"),
        P("dp", "tensor"),
    )
    out_specs = (P("dp", "tensor"), P("dp", "tensor"))

    def run(*args):
        return tuple(on_device(*args))

    return jax.shard_map(run, mesh=mesh, in_specs=in_specs, out_specs=out_specs, check_vma=False)
```

```python
import functools
import math

import jax
import jax.numpy as jnp
from jax import lax
from jax.experimental import pallas as pl
from jax.experimental.pallas import tpu as pltpu
from jax.sharding import PartitionSpec as P

MESH = pl.DeviceIdType.MESH
BF16 = jnp.bfloat16
F32 = jnp.float32


class Place:
    def __init__(self):
        self.d = lax.axis_index("dp")
        self.t = lax.axis_index("tensor")
        self.core = lax.rem(self.d, 2)
        self.q = lax.div(self.d, 2)
        self.z = lax.rem(self.q, 4)
        self.xh = lax.div(self.q, 4)
        self.y = lax.div(self.t, 2)
        self.xl = lax.rem(self.t, 2)

    def dev(self, dy=0, dx=0, dz=0, dh=0, dc=0):
        d = self.dp(dz, dh, dc)
        return (d, self.tensor(dy, dx))

    def tensor(self, dy=0, dx=0):
        return lax.rem(self.y + dy + 4, 4) * 2 + lax.rem(self.xl + dx, 2)

    def chip(self, dz=0, dh=0):
        return lax.rem(self.xh + dh, 2) * 4 + lax.rem(self.z + dz + 4, 4)

    def dp(self, dz=0, dh=0, dc=0):
        return self.chip(dz, dh) * 2 + lax.rem(self.core + dc, 2)


class Copies:
    def __init__(self, send, recv, local):
        self.send, self.recv, self.local = send, recv, local
        self.n = 0
        self.m = 0
        self.sent = []
        self.kept = []

    def remote(self, src, dst, to):
        c = pltpu.make_async_remote_copy(
            src_ref=src,
            dst_ref=dst,
            send_sem=self.send.at[self.n],
            recv_sem=self.recv.at[self.n],
            device_id=to,
            device_id_type=MESH,
        )
        self.n += 1
        c.start()
        self.sent.append(c)
        return c

    def keep(self, src, dst):
        c = pltpu.make_async_copy(src, dst, self.local.at[self.m])
        self.m += 1
        c.start()
        self.kept.append(c)
        return c

    def drain(self):
        for c in self.kept:
            c.wait()
        for c in self.sent:
            c.wait_send()


def barrier(devices):
    sem = pltpu.get_barrier_semaphore()
    for dev in devices:
        pl.semaphore_signal(sem, inc=1, device_id=dev, device_id_type=MESH)
    pl.semaphore_wait(sem, len(devices))


def columns(index, width):
    return pl.ds(pl.multiple_of(index * width, 128), width)


class Ring:
    def __init__(self, cp, to, own, place):
        self.cp, self.to, self.own, self.place = cp, to, own, place

    def start(self):
        send = lambda h, k: self.cp.remote(self.own(h), self.place(0, h), self.to(k))
        self.left0, self.right1 = send(0, 1), send(1, -1)
        self.left1, self.right0 = send(1, 1), send(0, -1)

    def turn(self):
        self.left0.wait_recv()
        self.far0 = self.cp.remote(self.place(-1, 0), self.place(-1, 0), self.to(1))
        self.right1.wait_recv()
        self.far1 = self.cp.remote(self.place(1, 1), self.place(1, 1), self.to(-1))

    def near(self):
        self.left1.wait_recv()
        self.right0.wait_recv()

    def far(self):
        self.far0.wait_recv()
        self.far1.wait_recv()


class Gather:
    def __init__(self, cp, me, own, place, own_part, part):
        self.cp, self.me, self.part, self.own_part = cp, me, part, own_part
        y = lambda k: me.dev(dy=k)
        self.rings = [
            Ring(cp, y, lambda h, p=p: own(p, h), lambda k, h, p=p: place(me.tensor(dy=k), p, h))
            for p in (0, 1)
        ]
        beside = lambda k, h: place(me.tensor(dy=k, dx=1), 0, h)
        self.beside = Ring(cp, y, lambda h: beside(0, h), beside)

    def to_x(self, k, src, p):
        ref = self.part(self.me.tensor(dy=k), p)
        return self.cp.remote(ref if src is None else src, ref, self.me.dev(dx=1))

    def start(self):
        self.x0 = self.to_x(0, self.own_part(0), 0)
        self.rings[1].start()
        self.rings[0].start()
        self.x1 = [self.to_x(0, self.own_part(1), 1)]

    def pass_on(self):
        self.x0.wait_recv()
        self.beside.start()
        self.rings[1].turn()
        self.rings[0].turn()
        self.rings[1].near()
        self.x1 += [self.to_x(k, None, 1) for k in (1, -1)]
        self.beside.turn()
        self.rings[1].far()
        self.x1.append(self.to_x(2, None, 1))

    def finish(self, done):
        me = self.me
        self.rings[0].near()
        done(me.tensor(dy=-1))
        done(me.tensor(dy=1))
        self.rings[0].far()
        done(me.tensor(dy=2))
        self.x1[0].wait_recv()
        done(me.tensor(dx=1))
        self.beside.near()
        self.x1[1].wait_recv()
        self.x1[2].wait_recv()
        done(me.tensor(dy=1, dx=1))
        done(me.tensor(dy=-1, dx=1))
        self.beside.far()
        self.x1[3].wait_recv()
        done(me.tensor(dy=2, dx=1))


def nothing(t):
    return None


def split(starts, lengths):
    return [[pl.ds(a, n), pl.ds(a + n, n)] for a, n in zip(starts, lengths)]


def hidden_and_down(h, d, hh, dd, send, recv, local):
    me = Place()
    cp = Copies(send, recv, local)
    piece = me.z * 2 + me.core
    others = ((0, 1), (1, 0), (3, 0), (2, 0), (1, 1), (3, 1), (2, 1))
    barrier(
        [me.dev(dy=a, dx=b) for a, b in others]
        + [me.dev(dz=1), me.dev(dz=-1), me.dev(dc=1)]
    )

    rows = pl.ds(pl.multiple_of(piece * 112, 16), 112)
    keep = cp.keep(d.at[rows, columns(me.t, 640)], dd.at[me.t, piece])
    handed = []
    for a, b in others:
        to = me.tensor(dy=a, dx=b)
        handed.append(
            cp.remote(d.at[rows, columns(to, 640)], dd.at[me.t, piece], me.dev(dy=a, dx=b))
        )
    cp.keep(h, hh.at[:, columns(me.t, 896)])

    half = split((0, 288), (144, 112))
    part = (pl.ds(0, 288), pl.ds(288, 224))
    gather = Gather(
        cp,
        me,
        lambda p, i: h.at[half[p][i]],
        lambda t, p, i: hh.at[half[p][i], columns(t, 896)],
        lambda p: h.at[part[p]],
        lambda t, p: hh.at[part[p], columns(t, 896)],
    )
    gather.start()
    keep.wait()
    cp.kept.remove(keep)
    for c in handed:
        c.wait_recv()
    there = lambda k: lax.rem(me.z + k + 4, 4) * 2 + me.core
    over = lambda k, i: dd.at[pl.ds(i * 4, 4), there(k)]
    ring = Ring(cp, lambda k: me.dev(dz=k), lambda i: over(0, i), over)
    ring.start()
    side = [cp.remote(dd.at[:, piece], dd.at[:, piece], me.dev(dc=1))]
    gather.pass_on()
    ring.turn()
    ring.near()
    for k in (1, -1):
        side.append(cp.remote(dd.at[:, there(k)], dd.at[:, there(k)], me.dev(dc=1)))
    ring.far()
    side.append(cp.remote(dd.at[:, there(2)], dd.at[:, there(2)], me.dev(dc=1)))
    gather.finish(nothing)
    for c in side:
        c.wait_recv()
    cp.drain()


def rows_and_weights(s, t, w, p, ss, tt, ww, pp, send, recv, local):
    me = Place()
    cp = Copies(send, recv, local)
    sibling = me.dev(dc=1)
    barrier(
        [me.dev(dy=1), me.dev(dy=-1), me.dev(dz=1), me.dev(dz=-1)]
        + [sibling, me.dev(dx=1), me.dev(dh=1)]
    )

    mine = columns(me.core, 256)
    other = columns(1 - me.core, 256)
    weights = ((w, ww), (p, pp))
    keeps = [cp.keep(a.at[:, mine], b.at[me.q, me.core]) for a, b in weights]
    swap = [cp.remote(a.at[:, other], b.at[me.q, me.core], sibling) for a, b in weights]
    s_half = split((0, 2304), (1152, 896))
    s_part = (pl.ds(0, 2304), pl.ds(2304, 1792))
    t_half = split((0, 288), (144, 112))
    t_part = (pl.ds(0, 288), pl.ds(288, 224))
    rows = Gather(
        cp,
        me,
        lambda a, i: s.at[:, s_half[a][i]],
        lambda b, a, i: ss.at[me.core, b, :, s_half[a][i]],
        lambda a: s.at[:, s_part[a]],
        lambda b, a: ss.at[me.core, b, :, s_part[a]],
    )
    teacher = Gather(
        cp,
        me,
        lambda a, i: t.at[t_half[a][i]],
        lambda b, a, i: tt.at[me.core, t_half[a][i], columns(b, 640)],
        lambda a: t.at[t_part[a]],
        lambda b, a: tt.at[me.core, t_part[a], columns(b, 640)],
    )
    rows.start()
    teacher.start()
    cp.keep(s, ss.at[me.core, me.t])
    cp.keep(t, tt.at[me.core, :, columns(me.t, 640)])
    side = [
        cp.remote(s, ss.at[me.core, me.t], sibling),
        cp.remote(t, tt.at[me.core, :, columns(me.t, 640)], sibling),
    ]
    for c in keeps:
        c.wait()
        cp.kept.remove(c)
    for c in swap:
        c.wait_recv()
    over = [cp.remote(b.at[me.q], b.at[me.q], me.dev(dh=1)) for a, b in weights]

    def ring(ref, dh):
        block = lambda k, i: ref.at[me.chip(dz=k, dh=dh), i]
        return Ring(cp, lambda k: me.dev(dz=k), lambda i: block(0, i), block)

    rings = [ring(b, 0) for a, b in weights]
    far = [ring(b, 1) for a, b in weights]
    for r in rings:
        r.start()
    rows.pass_on()
    for c, r in zip(over, far):
        c.wait_recv()
        r.start()
    teacher.pass_on()
    for r in rings + far:
        r.turn()

    def s_side(b):
        block = ss.at[me.core, b]
        side.append(cp.remote(block, block, sibling))

    def t_side(b):
        block = tt.at[me.core, :, columns(b, 640)]
        side.append(cp.remote(block, block, sibling))

    rows.finish(s_side)
    teacher.finish(t_side)
    for r in rings + far:
        r.near()
        r.far()
    for c in side:
        c.wait_recv()
    cp.drain()


def scatter_sums(factor, gw, gp, ow, op, rx, sx, rz, rw, sw, rh, tw, tp, send, recv, local):
    me = Place()
    cp = Copies(send, recv, local)
    across, sibling = me.dev(dh=1), me.dev(dc=1)
    barrier([me.dev(dz=k) for k in (1, 2, 3)] + [across, sibling])
    chunk = lambda g, width, **to: g.at[:, columns(me.chip(**to), width)]
    from_x, from_z = {}, {}
    for k in (2, 1, 3, 0):
        from_x[k] = cp.remote(chunk(gp, 640, dz=k, dh=1), rx.at[k], across)
    for h in (1, 0):
        for k in (2, 1, 3):
            from_z[h, k] = cp.remote(chunk(gw, 512, dz=k, dh=h), rw.at[h, k - 1], me.dev(dz=k))

    def total(mine, base, others, tile):
        out = mine[:, columns(base + tile, 128)].astype(F32)
        for r in others:
            out += r[:, tile * 128 : tile * 128 + 128].astype(F32)
        return out

    second = {}
    for k in (2, 1, 3):
        from_x[k].wait_recv()
        for i in range(5):
            sx[k - 1, :, i * 128 : i * 128 + 128] = total(
                gp, me.chip(dz=k) * 5, [rx.at[k]], i
            ).astype(BF16)
        second[k] = cp.remote(sx.at[k - 1], rz.at[k - 1], me.dev(dz=k))
    for k in (2, 1, 3):
        from_z[1, k].wait_recv()
    for i in range(4):
        sw[:, i * 128 : i * 128 + 128] = total(
            gw, me.chip(dh=1) * 4, [rw.at[1, k] for k in range(3)], i
        ).astype(BF16)
    back = cp.remote(sw, rh, across)

    mine = columns(me.core, 256)
    last = []

    def hand_out(g, staged, out, rows, others):
        tiles = rows // 64
        for i in range(tiles):
            value = total(g, me.q * tiles, others, i) * factor
            staged[i * 128 : i * 128 + 128, :] = value.T
        theirs = pl.ds(pl.multiple_of((1 - me.core) * rows, 64), rows)
        ours = pl.ds(pl.multiple_of(me.core * rows, 64), rows)
        last.append(cp.remote(staged.at[theirs], out.at[:, mine], sibling))
        cp.keep(staged.at[ours], out.at[:, mine])

    from_x[0].wait_recv()
    for k in (2, 1, 3):
        second[k].wait_recv()
    hand_out(gp, tp, op, 320, [rx.at[0]] + [rz.at[k] for k in range(3)])
    for k in (2, 1, 3):
        from_z[0, k].wait_recv()
    back.wait_recv()
    hand_out(gw, tw, ow, 256, [rw.at[0, k] for k in range(3)] + [rh])
    for c in last:
        c.wait_recv()
    cp.drain()


ANY = pl.BlockSpec(memory_space=pl.ANY)
VMEM = pl.BlockSpec(memory_space=pltpu.VMEM)


def dma(n):
    return pltpu.SemaphoreType.DMA((n,))


def call(kernel, ident, outs, args, copies, kept, scratch=(), spec=ANY):
    return pl.pallas_call(
        kernel,
        out_shape=[jax.ShapeDtypeStruct(shape, dtype) for shape, dtype in outs],
        in_specs=[spec] * len(args),
        out_specs=[spec] * len(outs),
        scratch_shapes=[*scratch, dma(copies), dma(copies), dma(kept)],
        compiler_params=pltpu.CompilerParams(
            collective_id=ident, has_side_effects=True, vmem_limit_bytes=48 * 2**20
        ),
    )(*args)


def dot(a, b, ca, cb):
    return lax.dot_general(a, b, (((ca,), (cb,)), ((), ())), preferred_element_type=F32)


def on_device(teacher_hidden, teacher_down, student_in, student_weight, projection):
    factor = 1.0 / math.sqrt(8192)
    hidden, down = call(
        hidden_and_down,
        1,
        [((512, 7168), BF16), ((8, 8, 112, 640), BF16)],
        (teacher_hidden, teacher_down),
        48,
        2,
    )
    block = dot(hidden, down.reshape(7168, 640), 1, 0).astype(BF16)
    rows, teacher, weight, proj = call(
        rows_and_weights,
        2,
        [((2, 8, 64, 4096), BF16), ((2, 512, 5120), BF16), ((8, 2, 256, 256), BF16), ((8, 2, 320, 256), BF16)],
        (student_in, block, student_weight, projection),
        96,
        4,
    )
    rows = rows.reshape(1024, 4096)
    teacher = teacher.reshape(1024, 5120)
    residual = (
        dot(rows, weight.reshape(4096, 256), 1, 0) - dot(teacher, proj.reshape(5120, 256), 1, 0)
    ).astype(BF16)
    grad_weight = dot(residual, rows, 0, 0).astype(BF16)
    grad_projection = dot(residual, teacher, 0, 0).astype(BF16)
    vmem = lambda *shape: pltpu.VMEM(shape, BF16)
    return call(
        functools.partial(scatter_sums, factor),
        3,
        [((256, 512), F32), ((320, 512), F32)],
        (grad_weight, grad_projection),
        16,
        2,
        (
            vmem(4, 256, 640),
            vmem(3, 256, 640),
            vmem(3, 256, 640),
            vmem(2, 3, 256, 512),
            vmem(256, 512),
            vmem(256, 512),
            pltpu.VMEM((512, 256), F32),
            pltpu.VMEM((640, 256), F32),
        ),
        VMEM,
    )


def solution(mesh):
    in_specs = (
        P("dp", "tensor"),
        P("tensor", None),
        P(("dp", "tensor"), None),
        P("dp", "tensor"),
        P("dp", "tensor"),
    )
    out_specs = (P("dp", "tensor"), P("dp", "tensor"))

    def run(*args):
        return tuple(on_device(*args))

    return jax.shard_map(run, mesh=mesh, in_specs=in_specs, out_specs=out_specs, check_vma=False)
```

```python
import functools
import math

import jax
import jax.numpy as jnp
from jax import lax
from jax.experimental import pallas as pl
from jax.experimental.pallas import tpu as pltpu
from jax.sharding import PartitionSpec as P

MESH = pl.DeviceIdType.MESH
BF16 = jnp.bfloat16
F32 = jnp.float32
COPIES = 152


class Place:
    def __init__(self):
        self.d = lax.axis_index("dp")
        self.t = lax.axis_index("tensor")
        self.core = lax.rem(self.d, 2)
        self.q = lax.div(self.d, 2)
        self.z = lax.rem(self.q, 4)
        self.xh = lax.div(self.q, 4)
        self.y = lax.div(self.t, 2)
        self.xl = lax.rem(self.t, 2)

    def dev(self, dy=0, dx=0, dz=0, dh=0, dc=0):
        d = self.dp(dz, dh, dc)
        return (d, self.tensor(dy, dx))

    def tensor(self, dy=0, dx=0):
        return lax.rem(self.y + dy + 4, 4) * 2 + lax.rem(self.xl + dx, 2)

    def chip(self, dz=0, dh=0):
        return lax.rem(self.xh + dh, 2) * 4 + lax.rem(self.z + dz + 4, 4)

    def dp(self, dz=0, dh=0, dc=0):
        return self.chip(dz, dh) * 2 + lax.rem(self.core + dc, 2)


class Copies:
    def __init__(self, send, recv, local):
        self.send, self.recv, self.local = send, recv, local
        self.n = 0
        self.m = 0
        self.sent = []
        self.kept = []

    def remote(self, src, dst, to):
        c = pltpu.make_async_remote_copy(
            src_ref=src,
            dst_ref=dst,
            send_sem=self.send.at[self.n],
            recv_sem=self.recv.at[self.n],
            device_id=to,
            device_id_type=MESH,
        )
        self.n += 1
        c.start()
        self.sent.append(c)
        return c

    def keep(self, src, dst):
        c = pltpu.make_async_copy(src, dst, self.local.at[self.m])
        self.m += 1
        c.start()
        self.kept.append(c)
        return c

    def kept_now(self, c):
        c.wait()
        self.kept = [k for k in self.kept if k is not c]

    def drain(self):
        for c in self.kept:
            c.wait()
        for c in self.sent:
            c.wait_send()


def barrier(devices):
    sem = pltpu.get_barrier_semaphore()
    for dev in devices:
        pl.semaphore_signal(sem, inc=1, device_id=dev, device_id_type=MESH)
    pl.semaphore_wait(sem, len(devices))


def columns(index, width):
    return pl.ds(pl.multiple_of(index * width, 128), width)


class Ring:
    def __init__(self, cp, to, own, place):
        self.cp, self.to, self.own, self.place = cp, to, own, place

    def start(self):
        send = lambda h, k: self.cp.remote(self.own(h), self.place(0, h), self.to(k))
        self.left0, self.right1 = send(0, 1), send(1, -1)
        self.left1, self.right0 = send(1, 1), send(0, -1)

    def turn(self):
        self.left0.wait_recv()
        self.far0 = self.cp.remote(self.place(-1, 0), self.place(-1, 0), self.to(1))
        self.right1.wait_recv()
        self.far1 = self.cp.remote(self.place(1, 1), self.place(1, 1), self.to(-1))

    def near(self):
        self.left1.wait_recv()
        self.right0.wait_recv()

    def far(self):
        self.far0.wait_recv()
        self.far1.wait_recv()


class Gather:
    def __init__(self, cp, me, own, place, own_part, part):
        self.cp, self.me, self.part, self.own_part = cp, me, part, own_part
        y = lambda k: me.dev(dy=k)
        self.rings = [
            Ring(cp, y, lambda h, p=p: own(p, h), lambda k, h, p=p: place(me.tensor(dy=k), p, h))
            for p in (0, 1)
        ]
        beside = lambda k, h: place(me.tensor(dy=k, dx=1), 0, h)
        self.beside = Ring(cp, y, lambda h: beside(0, h), beside)

    def to_x(self, k, src, p):
        ref = self.part(self.me.tensor(dy=k), p)
        return self.cp.remote(ref if src is None else src, ref, self.me.dev(dx=1))

    def start(self):
        self.x0 = self.to_x(0, self.own_part(0), 0)
        self.rings[1].start()
        self.rings[0].start()
        self.x1 = [self.to_x(0, self.own_part(1), 1)]

    def pass_on(self):
        self.x0.wait_recv()
        self.beside.start()
        self.rings[1].turn()
        self.rings[0].turn()
        self.rings[1].near()
        self.x1 += [self.to_x(k, None, 1) for k in (1, -1)]
        self.beside.turn()
        self.rings[1].far()
        self.x1.append(self.to_x(2, None, 1))

    def finish(self, done):
        me = self.me
        self.rings[0].near()
        done(me.tensor(dy=-1))
        done(me.tensor(dy=1))
        self.rings[0].far()
        done(me.tensor(dy=2))

    def finish_beside(self, done):
        me = self.me
        self.x1[0].wait_recv()
        done(me.tensor(dx=1))
        self.beside.near()
        self.x1[1].wait_recv()
        self.x1[2].wait_recv()
        done(me.tensor(dy=1, dx=1))
        done(me.tensor(dy=-1, dx=1))
        self.beside.far()
        self.x1[3].wait_recv()
        done(me.tensor(dy=2, dx=1))


def nothing(t):
    return None


def split(starts, lengths):
    return [[pl.ds(a, n), pl.ds(a + n, n)] for a, n in zip(starts, lengths)]


def dot(a, b):
    return jnp.dot(a, b, preferred_element_type=F32)


def distill(
    factor,
    h, d, s, w, p,
    ow, op,
    hh, dd, ss, tt, ww, pp, tacc, racc, rest,
    gx, gp, gw, rx, sx, rz, rw, sw, rh, tw, tp,
    send, recv, local,
):
    me = Place()
    cp = Copies(send, recv, local)
    sibling, across = me.dev(dc=1), me.dev(dh=1)
    others = ((0, 1), (1, 0), (3, 0), (2, 0), (1, 1), (3, 1), (2, 1))
    barrier(
        [me.dev(dy=a, dx=b) for a, b in others]
        + [me.dev(dz=k) for k in (1, 3, 2)]
        + [sibling, across]
    )

    piece = me.z * 2 + me.core
    rows = pl.ds(pl.multiple_of(piece * 112, 16), 112)
    first = [cp.keep(d.at[rows, columns(me.t, 640)], dd.at[me.t, piece])]
    handed = []
    for a, b in others:
        to = me.tensor(dy=a, dx=b)
        handed.append(
            cp.remote(d.at[rows, columns(to, 640)], dd.at[me.t, piece], me.dev(dy=a, dx=b))
        )
    hidden_keep = cp.keep(h, hh.at[:, columns(me.t, 896)])
    half = split((0, 288), (144, 112))
    part = (pl.ds(0, 288), pl.ds(288, 224))
    hidden = Gather(
        cp,
        me,
        lambda p, i: h.at[half[p][i]],
        lambda t, p, i: hh.at[half[p][i], columns(t, 896)],
        lambda p: h.at[part[p]],
        lambda t, p: hh.at[part[p], columns(t, 896)],
    )
    hidden.start()

    mine, other = columns(me.core, 256), columns(1 - me.core, 256)
    weights = ((w, ww, 256), (p, pp, 320))
    at = lambda q, c, n: pl.ds(pl.multiple_of((q * 2 + c) * n, 64), n)
    pair = lambda q, n: pl.ds(pl.multiple_of(q * 2 * n, 128), 2 * n)
    first += [cp.keep(a.at[:, mine], b.at[at(me.q, me.core, n)]) for a, b, n in weights]
    swap = [
        cp.remote(a.at[:, other], b.at[at(me.q, me.core, n)], sibling) for a, b, n in weights
    ]

    for c in first:
        cp.kept_now(c)
    for c in handed:
        c.wait_recv()
    there = lambda k: lax.rem(me.z + k + 4, 4) * 2 + me.core
    over = lambda k, i: dd.at[pl.ds(i * 4, 4), there(k)]
    down = Ring(cp, lambda k: me.dev(dz=k), lambda i: over(0, i), over)
    down.start()
    down_side = []

    def pass_down(k):
        block = dd.at[:, there(k)]
        down_side.append(cp.remote(block, block, sibling))

    pass_down(0)
    hidden.pass_on()

    s_half = split((0, 2304), (1152, 896))
    s_part = (pl.ds(0, 2304), pl.ds(2304, 1792))
    s_rows = lambda b: pl.ds(pl.multiple_of((me.core * 8 + b) * 64, 64), 64)
    student = Gather(
        cp,
        me,
        lambda a, i: s.at[:, s_half[a][i]],
        lambda b, a, i: ss.at[s_rows(b), s_half[a][i]],
        lambda a: s.at[:, s_part[a]],
        lambda b, a: ss.at[s_rows(b), s_part[a]],
    )
    student.start()
    student_keep = cp.keep(s, ss.at[s_rows(me.t)])
    student_side = [cp.remote(s, ss.at[s_rows(me.t)], sibling)]
    for c in swap:
        c.wait_recv()
    far_weights = [
        cp.remote(b.at[pair(me.q, n)], b.at[pair(me.q, n)], across) for a, b, n in weights
    ]
    down.turn()
    down.near()
    pass_down(1)
    pass_down(-1)

    def ring(ref, n, dh):
        block = lambda k, i: ref.at[at(me.chip(dz=k, dh=dh), i, n)]
        return Ring(cp, lambda k: me.dev(dz=k), lambda i: block(0, i), block)

    near_rings = [ring(b, n, 0) for a, b, n in weights]
    far_rings = [ring(b, n, 1) for a, b, n in weights]
    for r in near_rings:
        r.start()
    down.far()
    pass_down(2)

    tacc[...] = jnp.zeros_like(tacc)

    def teacher_blocks(dx):
        @pl.loop(0, 4)
        def _(k):
            b = me.tensor(dy=k, dx=dx)
            left = hh[:, columns(b, 896)]
            right = dd.at[b]
            for n in (slice(0, 256), slice(256, 512), slice(512, 640)):
                tacc[:, n] += dot(left, right[:, :, n].reshape(896, n.stop - n.start))

    cp.kept_now(hidden_keep)
    hidden.finish(nothing)
    for c in down_side:
        c.wait_recv()
    teacher_blocks(0)
    hidden.finish_beside(nothing)
    teacher_blocks(1)
    half_rows = lambda c: pl.multiple_of(c * 512, 512)
    own_rows = half_rows(me.core)
    own_block = tt.at[pl.ds(own_rows, 512), columns(me.t, 640)]
    own_block[...] = tacc[...].astype(BF16)

    def t_rows(r):
        return pl.ds(pl.multiple_of(own_rows + r.start, 16), r.size)

    teacher = Gather(
        cp,
        me,
        lambda a, i: tt.at[t_rows(half[a][i]), columns(me.t, 640)],
        lambda b, a, i: tt.at[t_rows(half[a][i]), columns(b, 640)],
        lambda a: tt.at[t_rows(part[a]), columns(me.t, 640)],
        lambda b, a: tt.at[t_rows(part[a]), columns(b, 640)],
    )
    teacher.start()
    teacher_side = [cp.remote(own_block, own_block, sibling)]
    student.pass_on()
    for c, r in zip(far_weights, far_rings):
        c.wait_recv()
        r.start()
    for r in near_rings + far_rings:
        r.turn()

    def pass_student(b):
        block = ss.at[s_rows(b)]
        student_side.append(cp.remote(block, block, sibling))

    student.finish(pass_student)
    teacher.pass_on()
    student.finish_beside(pass_student)
    for r in near_rings + far_rings:
        r.near()
        r.far()
    cp.kept_now(student_keep)
    for c in student_side:
        c.wait_recv()

    racc[...] = jnp.zeros_like(racc)

    @pl.loop(0, 8)
    def _(k):
        depth = pl.ds(pl.multiple_of(k * 512, 512), 512)
        racc[...] += dot(ss[:, depth], ww[depth, :])

    def target(core, b):
        at_rows = pl.ds(half_rows(core), 512)
        weight = pp[pl.ds(pl.multiple_of(b * 640, 128), 640), :]
        racc[at_rows, :] -= dot(tt[at_rows, columns(b, 640)], weight)

    order = [me.t]
    target(me.core, me.t)

    def pass_teacher(b):
        block = tt.at[pl.ds(own_rows, 512), columns(b, 640)]
        teacher_side.append(cp.remote(block, block, sibling))
        order.append(b)
        target(me.core, b)
        teacher_side[len(order) - 2].wait_recv()
        target(1 - me.core, order[-2])

    teacher.finish(pass_teacher)
    teacher.finish_beside(pass_teacher)
    teacher_side[-1].wait_recv()
    target(1 - me.core, order[-1])
    for i in range(8):
        block = slice(i * 128, i * 128 + 128)
        rest[:, block] = racc[block, :].T.astype(BF16)

    def project(**to):
        return dot(rest[...], tt[:, columns(me.chip(**to), 640)])

    def weigh(**to):
        return dot(rest[...], ss[:, columns(me.chip(**to), 512)])

    from_x, from_z = {}, {}
    for k in (2, 1, 3, 0):
        gx[k] = project(dz=k, dh=1).astype(BF16)
        from_x[k] = cp.remote(gx.at[k], rx.at[k], across)
    for g in (1, 0):
        for k in (2, 1, 3):
            gw[g, k] = weigh(dz=k, dh=g).astype(BF16)
            from_z[g, k] = cp.remote(gw.at[g, k], rw.at[g, k - 1], me.dev(dz=k))
    second = {}
    for k in (2, 1, 3):
        gp[...] = project(dz=k)
        from_x[k].wait_recv()
        sx[k - 1] = (gp[...] + rx[k].astype(F32)).astype(BF16)
        second[k] = cp.remote(sx.at[k - 1], rz.at[k - 1], me.dev(dz=k))
    gp[:, :512] = weigh(dh=1)
    for k in (2, 1, 3):
        from_z[1, k].wait_recv()
    sw[...] = (
        gp[:, :512] + rw[1, 0].astype(F32) + rw[1, 1].astype(F32) + rw[1, 2].astype(F32)
    ).astype(BF16)
    back = cp.remote(sw, rh, across)
    last = []

    def hand_out(staged, out, n, parts):
        for i in range(n // 64):
            block = slice(i * 128, i * 128 + 128)
            value = gp[:, block]
            for r in parts:
                value += r[:, block].astype(F32)
            staged[block, :] = (value * factor).T
        theirs = pl.ds(pl.multiple_of((1 - me.core) * n, 64), n)
        ours = pl.ds(pl.multiple_of(me.core * n, 64), n)
        last.append(cp.remote(staged.at[theirs], out.at[:, mine], sibling))
        cp.keep(staged.at[ours], out.at[:, mine])

    gp[...] = project()
    from_x[0].wait_recv()
    for k in (2, 1, 3):
        second[k].wait_recv()
    hand_out(tp, op, 320, [rx.at[0]] + [rz.at[k] for k in range(3)])
    gp[:, :512] = weigh()
    for k in (2, 1, 3):
        from_z[0, k].wait_recv()
    back.wait_recv()
    hand_out(tw, ow, 256, [rw.at[0, k] for k in range(3)] + [rh])
    for c in last:
        c.wait_recv()
    cp.drain()


def on_device(*args):
    narrow = lambda *shape: pltpu.VMEM(shape, BF16)
    wide = lambda *shape: pltpu.VMEM(shape, F32)
    return tuple(
        pl.pallas_call(
            functools.partial(distill, 1.0 / math.sqrt(8192)),
            out_shape=[
                jax.ShapeDtypeStruct((256, 512), F32),
                jax.ShapeDtypeStruct((320, 512), F32),
            ],
            in_specs=[pl.BlockSpec(memory_space=pl.ANY)] * 5,
            out_specs=[pl.BlockSpec(memory_space=pltpu.VMEM)] * 2,
            scratch_shapes=[
                narrow(512, 7168),
                narrow(8, 8, 112, 640),
                narrow(1024, 4096),
                narrow(1024, 5120),
                narrow(4096, 256),
                narrow(5120, 256),
                wide(512, 640),
                wide(1024, 256),
                narrow(256, 1024),
                narrow(4, 256, 640),
                wide(256, 640),
                narrow(2, 4, 256, 512),
                narrow(4, 256, 640),
                narrow(3, 256, 640),
                narrow(3, 256, 640),
                narrow(2, 3, 256, 512),
                narrow(256, 512),
                narrow(256, 512),
                wide(512, 256),
                wide(640, 256),
                pltpu.SemaphoreType.DMA((COPIES,)),
                pltpu.SemaphoreType.DMA((COPIES,)),
                pltpu.SemaphoreType.DMA((8,)),
            ],
            compiler_params=pltpu.CompilerParams(
                collective_id=1, has_side_effects=True, vmem_limit_bytes=62 * 2**20
            ),
        )(*args)
    )


def solution(mesh):
    in_specs = (
        P("dp", "tensor"),
        P("tensor", None),
        P(("dp", "tensor"), None),
        P("dp", "tensor"),
        P("dp", "tensor"),
    )
    out_specs = (P("dp", "tensor"), P("dp", "tensor"))

    return jax.shard_map(
        on_device, mesh=mesh, in_specs=in_specs, out_specs=out_specs, check_vma=False
    )
```

```python
import functools
import math

import jax
import jax.numpy as jnp
from jax import lax
from jax.experimental import pallas as pl
from jax.experimental.pallas import tpu as pltpu
from jax.sharding import PartitionSpec as P

MESH = pl.DeviceIdType.MESH
BF16 = jnp.bfloat16
F32 = jnp.float32
COPIES = 208
STEPS = 4
VMEM_MIB = 56
STEP = 512 // STEPS


class Place:
    def __init__(self):
        self.d = lax.axis_index("dp")
        self.t = lax.axis_index("tensor")
        self.core = lax.rem(self.d, 2)
        self.q = lax.div(self.d, 2)
        self.z = lax.rem(self.q, 4)
        self.xh = lax.div(self.q, 4)
        self.y = lax.div(self.t, 2)
        self.xl = lax.rem(self.t, 2)

    def dev(self, dy=0, dx=0, dz=0, dh=0, dc=0):
        d = self.dp(dz, dh, dc)
        return (d, self.tensor(dy, dx))

    def tensor(self, dy=0, dx=0):
        return lax.rem(self.y + dy + 4, 4) * 2 + lax.rem(self.xl + dx, 2)

    def chip(self, dz=0, dh=0):
        return lax.rem(self.xh + dh, 2) * 4 + lax.rem(self.z + dz + 4, 4)

    def dp(self, dz=0, dh=0, dc=0):
        return self.chip(dz, dh) * 2 + lax.rem(self.core + dc, 2)


class Copies:
    def __init__(self, send, recv, local):
        self.send, self.recv, self.local = send, recv, local
        self.n = 0
        self.m = 0
        self.sent = []
        self.kept = []

    def remote(self, src, dst, to):
        c = pltpu.make_async_remote_copy(
            src_ref=src,
            dst_ref=dst,
            send_sem=self.send.at[self.n],
            recv_sem=self.recv.at[self.n],
            device_id=to,
            device_id_type=MESH,
        )
        self.n += 1
        c.start()
        self.sent.append(c)
        return c

    def keep(self, src, dst):
        c = pltpu.make_async_copy(src, dst, self.local.at[self.m])
        self.m += 1
        c.start()
        self.kept.append(c)
        return c

    def kept_now(self, c):
        c.wait()
        self.kept = [k for k in self.kept if k is not c]

    def drain(self):
        for c in self.kept:
            c.wait()
        for c in self.sent:
            c.wait_send()


def barrier(devices):
    sem = pltpu.get_barrier_semaphore()
    for dev in devices:
        pl.semaphore_signal(sem, inc=1, device_id=dev, device_id_type=MESH)
    pl.semaphore_wait(sem, len(devices))


def columns(index, width):
    return pl.ds(pl.multiple_of(index * width, 128), width)


class Ring:
    def __init__(self, cp, to, own, place):
        self.cp, self.to, self.own, self.place = cp, to, own, place

    def start(self):
        send = lambda h, k: self.cp.remote(self.own(h), self.place(0, h), self.to(k))
        self.left0, self.right1 = send(0, 1), send(1, -1)
        self.left1, self.right0 = send(1, 1), send(0, -1)

    def start_half(self, h):
        send = lambda k: self.cp.remote(self.own(h), self.place(0, h), self.to(k))
        if h == 0:
            self.left0, self.right0 = send(1), send(-1)
        else:
            self.right1, self.left1 = send(-1), send(1)

    def turn(self):
        self.left0.wait_recv()
        self.far0 = self.cp.remote(self.place(-1, 0), self.place(-1, 0), self.to(1))
        self.right1.wait_recv()
        self.far1 = self.cp.remote(self.place(1, 1), self.place(1, 1), self.to(-1))

    def near(self):
        self.left1.wait_recv()
        self.right0.wait_recv()

    def far(self):
        self.far0.wait_recv()
        self.far1.wait_recv()


def dot(a, b):
    return jnp.dot(a, b, preferred_element_type=F32)


def distill(
    factor,
    h, d, s, w, p,
    ow, op,
    hh, dd, ss, tt, ww, pp, part, theirs, came, racc, rest,
    gx, gp, gw, rx, sx, rz, rw, sw, rh, tw, tp,
    send, recv, local,
):
    me = Place()
    cp = Copies(send, recv, local)
    sibling, across, beside = me.dev(dc=1), me.dev(dh=1), me.dev(dx=1)
    to_y, to_z = lambda k: me.dev(dy=k), lambda k: me.dev(dz=k)
    barrier(
        [to_y(k) for k in (1, 3, 2)] + [to_z(k) for k in (1, 3, 2)] + [sibling, across, beside]
    )

    piece = me.z * 2 + me.core
    wide = lambda k: columns(lax.rem(me.y + k, 4), 1280)
    rows = pl.ds(pl.multiple_of(piece * 112, 16), 112)
    handed = [[], []]
    for i in (0, 1):
        for k in (2, 1, 3):
            half = columns(lax.rem(me.y + k, 4) * 2 + i, 640)
            to = dd.at[4 - k, piece, :, pl.ds(i * 640, 640)]
            handed[i].append(cp.remote(d.at[rows, half], to, to_y(k)))
    at_hidden = lambda k: columns(lax.rem(me.y + k + 4, 4), 896)
    hidden = Ring(
        cp,
        to_y,
        lambda i: h.at[pl.ds(i * 256, 256)],
        lambda k, i: hh.at[pl.ds(i * 256, 256), at_hidden(k)],
    )

    s_rows = lambda b: pl.ds(pl.multiple_of((me.core * 8 + b) * 64, 64), 64)

    def student_ring(dx):
        def place(k, i):
            return ss.at[s_rows(me.tensor(dy=k, dx=dx)), pl.ds(i * 2048, 2048)]

        own = (lambda i: place(0, i)) if dx else (lambda i: s.at[:, pl.ds(i * 2048, 2048)])
        return Ring(cp, to_y, own, place)

    student, student_beside = student_ring(0), student_ring(1)
    student_x = cp.remote(s, ss.at[s_rows(me.t)], beside)
    student_side = [cp.remote(s, ss.at[s_rows(me.t)], sibling)]

    def student_over_core(k, dx):
        block = ss.at[s_rows(me.tensor(dy=k, dx=dx))]
        student_side.append(cp.remote(block, block, sibling))

    mine, other = columns(me.core, 256), columns(1 - me.core, 256)
    weights = ((w, ww, 256), (p, pp, 320))
    at = lambda q, c, n: pl.ds(pl.multiple_of((q * 2 + c) * n, 64), n)
    pair = lambda q, n: pl.ds(pl.multiple_of(q * 2 * n, 128), 2 * n)
    swap = [
        cp.remote(a.at[:, other], b.at[at(me.q, me.core, n)], sibling) for a, b, n in weights
    ]
    own_weights = [cp.keep(a.at[:, mine], b.at[at(me.q, me.core, n)]) for a, b, n in weights]

    own_teacher = [cp.keep(h, hh.at[:, at_hidden(0)])]
    for i in range(8):
        own_teacher.append(cp.keep(d.at[pl.ds(i * 112, 112), wide(0)], dd.at[0, i]))
    own_student = cp.keep(s, ss.at[s_rows(me.t)])

    for c in own_weights:
        cp.kept_now(c)
    for c in swap:
        c.wait_recv()

    def ring(ref, n, dh):
        block = lambda k, i: ref.at[at(me.chip(dz=k, dh=dh), i, n)]
        return Ring(cp, to_z, lambda i: block(0, i), block)

    weight_rings = [ring(b, n, 0) for a, b, n in weights]
    far_rings = [ring(b, n, 1) for a, b, n in weights]
    far_weights = [
        cp.remote(b.at[pair(me.q, n)], b.at[pair(me.q, n)], across) for a, b, n in weights
    ]
    there = lambda k: lax.rem(me.z + k + 4, 4) * 2 + me.core
    over = lambda k, i: dd.at[1:4, there(k), :, pl.ds(i * 640, 640)]
    down = Ring(cp, to_z, lambda i: over(0, i), over)
    for c in handed[0]:
        c.wait_recv()
    down.start_half(0)
    hidden.start()
    for c in handed[1]:
        c.wait_recv()
    down.start_half(1)
    down_side = []

    def pass_down(k):
        block = dd.at[1:4, there(k)]
        down_side.append(cp.remote(block, block, sibling))

    pass_down(0)

    def teacher_block(out, dx, j):
        left = hh[:, columns(lax.rem(me.y + j, 4), 896)]
        for n in ((0, 256), (256, 256), (512, 128)):
            at_n = pl.ds(pl.multiple_of(lax.rem(me.xl + dx, 2) * 640 + n[0], 128), n[1])
            right = dd[j, :, :, at_n].reshape(896, n[1])
            to = slice(n[0], n[0] + n[1])
            if isinstance(j, int):
                out[:, to] = dot(left, right)
            else:
                out[:, to] += dot(left, right)

    for c in own_teacher:
        cp.kept_now(c)
    teacher_block(theirs, 1, 0)
    teacher_block(part, 0, 0)

    down.turn()
    hidden.turn()
    down.near()
    pass_down(1)
    pass_down(-1)
    down.far()
    pass_down(2)
    for r in weight_rings:
        r.start()
    student_x.wait_recv()
    student.start()
    student_beside.start()
    hidden.near()
    hidden.far()
    for c in down_side:
        c.wait_recv()

    @pl.loop(1, 4)
    def _(j):
        teacher_block(theirs, 1, j)

    chunk = lambda r: pl.ds(r * STEP, STEP)
    partial = [cp.remote(theirs.at[chunk(r)], came.at[chunk(r)], beside) for r in range(STEPS)]

    @pl.loop(1, 4)
    def _(j):
        teacher_block(part, 0, j)

    base = me.core * 512

    def t_block(r, k, dx, i=None):
        n = STEP if i is None else STEP // 2
        row = pl.multiple_of(base + r * STEP + (i or 0) * n, 16)
        return tt.at[pl.ds(row, n), columns(me.tensor(dy=k, dx=dx), 640)]

    def teacher_ring(r, dx):
        place = lambda k, i: t_block(r, k, dx, i)
        return Ring(cp, to_y, lambda i: place(0, i), place)

    rings = [[teacher_ring(r, dx) for dx in (0, 1)] for r in range(STEPS)]
    over_x = {}
    side = [[] for r in range(STEPS)]

    def over_core(r, k, dx):
        side[r].append(cp.remote(t_block(r, k, dx), t_block(r, k, dx), sibling))

    def summed(r):
        partial[r].wait_recv()
        t_block(r, 0, 0)[...] = (part[chunk(r), :] + came[chunk(r), :]).astype(BF16)
        over_x[r] = cp.remote(t_block(r, 0, 0), t_block(r, 0, 0), beside)
        rings[r][0].start()
        over_core(r, 0, 0)

    def exchanged(r):
        over_x[r].wait_recv()
        rings[r][1].start()
        over_core(r, 0, 1)

    def arrived(r):
        for dx in (0, 1):
            rings[r][dx].near()
            over_core(r, 1, dx)
            over_core(r, -1, dx)
            rings[r][dx].far()
            over_core(r, 2, dx)

    def student_output():
        for dx, r in ((0, student), (1, student_beside)):
            r.near()
            r.far()
            for k in (1, -1, 2):
                student_over_core(k, dx)
        student_over_core(0, 1)
        for r in weight_rings + far_rings:
            r.near()
            r.far()
        cp.kept_now(own_student)
        for c in student_side:
            c.wait_recv()

        @pl.loop(0, 4)
        def _(k):
            rows = pl.ds(pl.multiple_of(k * 256, 256), 256)
            racc[rows, :] = dot(ss[rows, :], ww[...])

    def residual(r):
        for c in side[r]:
            c.wait_recv()
        both = [slice(c * 512 + r * STEP, c * 512 + (r + 1) * STEP) for c in (0, 1)]
        target = dot(jnp.concatenate([tt[rows, :] for rows in both], axis=0), pp[...])
        for c, rows in enumerate(both):
            value = racc[rows, :] - target[c * STEP : (c + 1) * STEP, :]
            rest[:, rows] = value.T.astype(BF16)

    for step in range(STEPS + 3):
        if step < STEPS:
            summed(step)
        if 1 <= step <= STEPS:
            exchanged(step - 1)
            rings[step - 1][0].turn()
        if 2 <= step < STEPS + 2:
            rings[step - 2][1].turn()
        if step == 0:
            student.turn()
            student_beside.turn()
            for r in weight_rings:
                r.turn()
            for c, r in zip(far_weights, far_rings):
                c.wait_recv()
                r.start()
        if step == 2:
            for r in far_rings:
                r.turn()
        if step >= 3:
            arrived(step - 3)
        if step == STEPS:
            student_output()
        if step > STEPS:
            residual(step - STEPS - 1)
    for r in range(2, STEPS):
        residual(r)

    def project(**to):
        return dot(rest[...], tt[:, columns(me.chip(**to), 640)])

    def weigh(**to):
        return dot(rest[...], ss[:, columns(me.chip(**to), 512)])

    from_x, from_z = {}, {}
    for k in (2, 1, 3, 0):
        gx[k] = project(dz=k, dh=1).astype(BF16)
        from_x[k] = cp.remote(gx.at[k], rx.at[k], across)
    for g in (1, 0):
        for k in (2, 1, 3):
            gw[g, k] = weigh(dz=k, dh=g).astype(BF16)
            from_z[g, k] = cp.remote(gw.at[g, k], rw.at[g, k - 1], me.dev(dz=k))
    second = {}
    for k in (2, 1, 3):
        gp[...] = project(dz=k)
        from_x[k].wait_recv()
        sx[k - 1] = (gp[...] + rx[k].astype(F32)).astype(BF16)
        second[k] = cp.remote(sx.at[k - 1], rz.at[k - 1], me.dev(dz=k))
    gp[:, :512] = weigh(dh=1)
    for k in (2, 1, 3):
        from_z[1, k].wait_recv()
    sw[...] = (
        gp[:, :512] + rw[1, 0].astype(F32) + rw[1, 1].astype(F32) + rw[1, 2].astype(F32)
    ).astype(BF16)
    back = cp.remote(sw, rh, across)
    last = []

    def hand_out(staged, out, n, parts):
        for i in range(n // 64):
            block = slice(i * 128, i * 128 + 128)
            value = gp[:, block]
            for r in parts:
                value += r[:, block].astype(F32)
            staged[block, :] = (value * factor).T
        theirs = pl.ds(pl.multiple_of((1 - me.core) * n, 64), n)
        ours = pl.ds(pl.multiple_of(me.core * n, 64), n)
        last.append(cp.remote(staged.at[theirs], out.at[:, mine], sibling))
        cp.keep(staged.at[ours], out.at[:, mine])

    gp[...] = project()
    from_x[0].wait_recv()
    for k in (2, 1, 3):
        second[k].wait_recv()
    hand_out(tp, op, 320, [rx.at[0]] + [rz.at[k] for k in range(3)])
    gp[:, :512] = weigh()
    for k in (2, 1, 3):
        from_z[0, k].wait_recv()
    back.wait_recv()
    hand_out(tw, ow, 256, [rw.at[0, k] for k in range(3)] + [rh])
    for c in last:
        c.wait_recv()
    cp.drain()


def on_device(*args):
    narrow = lambda *shape: pltpu.VMEM(shape, BF16)
    wide = lambda *shape: pltpu.VMEM(shape, F32)
    return tuple(
        pl.pallas_call(
            functools.partial(distill, 1.0 / math.sqrt(8192)),
            out_shape=[
                jax.ShapeDtypeStruct((256, 512), F32),
                jax.ShapeDtypeStruct((320, 512), F32),
            ],
            in_specs=[pl.BlockSpec(memory_space=pl.ANY)] * 5,
            out_specs=[pl.BlockSpec(memory_space=pltpu.VMEM)] * 2,
            scratch_shapes=[
                narrow(512, 3584),
                narrow(4, 8, 112, 1280),
                narrow(1024, 4096),
                narrow(1024, 5120),
                narrow(4096, 256),
                narrow(5120, 256),
                wide(512, 640),
                wide(512, 640),
                wide(512, 640),
                wide(1024, 256),
                narrow(256, 1024),
                narrow(4, 256, 640),
                wide(256, 640),
                narrow(2, 4, 256, 512),
                narrow(4, 256, 640),
                narrow(3, 256, 640),
                narrow(3, 256, 640),
                narrow(2, 3, 256, 512),
                narrow(256, 512),
                narrow(256, 512),
                wide(512, 256),
                wide(640, 256),
                pltpu.SemaphoreType.DMA((COPIES,)),
                pltpu.SemaphoreType.DMA((COPIES,)),
                pltpu.SemaphoreType.DMA((16,)),
            ],
            compiler_params=pltpu.CompilerParams(
                collective_id=1, has_side_effects=True, vmem_limit_bytes=VMEM_MIB * 2**20
            ),
        )(*args)
    )


def solution(mesh):
    in_specs = (
        P("dp", "tensor"),
        P("tensor", None),
        P(("dp", "tensor"), None),
        P("dp", "tensor"),
        P("dp", "tensor"),
    )
    out_specs = (P("dp", "tensor"), P("dp", "tensor"))

    return jax.shard_map(
        on_device, mesh=mesh, in_specs=in_specs, out_specs=out_specs, check_vma=False
    )
```

```python
import functools
import math

import jax
import jax.numpy as jnp
from jax import lax
from jax.experimental import pallas as pl
from jax.experimental.pallas import tpu as pltpu
from jax.sharding import PartitionSpec as P

MESH = pl.DeviceIdType.MESH
BF16 = jnp.bfloat16
F32 = jnp.float32
COPIES = 208
STEPS = 4
VMEM_MIB = 56
STEP = 512 // STEPS


class Place:
    def __init__(self):
        self.d = lax.axis_index("dp")
        self.t = lax.axis_index("tensor")
        self.core = lax.rem(self.d, 2)
        self.q = lax.div(self.d, 2)
        self.z = lax.rem(self.q, 4)
        self.xh = lax.div(self.q, 4)
        self.y = lax.div(self.t, 2)
        self.xl = lax.rem(self.t, 2)

    def dev(self, dy=0, dx=0, dz=0, dh=0, dc=0):
        d = self.dp(dz, dh, dc)
        return (d, self.tensor(dy, dx))

    def tensor(self, dy=0, dx=0):
        return lax.rem(self.y + dy + 4, 4) * 2 + lax.rem(self.xl + dx, 2)

    def chip(self, dz=0, dh=0):
        return lax.rem(self.xh + dh, 2) * 4 + lax.rem(self.z + dz + 4, 4)

    def dp(self, dz=0, dh=0, dc=0):
        return self.chip(dz, dh) * 2 + lax.rem(self.core + dc, 2)


class Copies:
    def __init__(self, send, recv, local):
        self.send, self.recv, self.local = send, recv, local
        self.n = 0
        self.m = 0
        self.sent = []
        self.kept = []

    def remote(self, src, dst, to):
        c = pltpu.make_async_remote_copy(
            src_ref=src,
            dst_ref=dst,
            send_sem=self.send.at[self.n],
            recv_sem=self.recv.at[self.n],
            device_id=to,
            device_id_type=MESH,
        )
        self.n += 1
        c.start()
        self.sent.append(c)
        return c

    def keep(self, src, dst):
        c = pltpu.make_async_copy(src, dst, self.local.at[self.m])
        self.m += 1
        c.start()
        self.kept.append(c)
        return c

    def kept_now(self, c):
        c.wait()
        self.kept = [k for k in self.kept if k is not c]

    def drain(self):
        for c in self.kept:
            c.wait()
        for c in self.sent:
            c.wait_send()


def barrier(devices):
    sem = pltpu.get_barrier_semaphore()
    for dev in devices:
        pl.semaphore_signal(sem, inc=1, device_id=dev, device_id_type=MESH)
    pl.semaphore_wait(sem, len(devices))


def columns(index, width):
    return pl.ds(pl.multiple_of(index * width, 128), width)


class Ring:
    def __init__(self, cp, to, own, place):
        self.cp, self.to, self.own, self.place = cp, to, own, place

    def start(self):
        send = lambda h, k: self.cp.remote(self.own(h), self.place(0, h), self.to(k))
        self.left0, self.right1 = send(0, 1), send(1, -1)
        self.left1, self.right0 = send(1, 1), send(0, -1)

    def start_half(self, h):
        send = lambda k: self.cp.remote(self.own(h), self.place(0, h), self.to(k))
        if h == 0:
            self.left0, self.right0 = send(1), send(-1)
        else:
            self.right1, self.left1 = send(-1), send(1)

    def turn(self):
        self.left0.wait_recv()
        self.far0 = self.cp.remote(self.place(-1, 0), self.place(-1, 0), self.to(1))
        self.right1.wait_recv()
        self.far1 = self.cp.remote(self.place(1, 1), self.place(1, 1), self.to(-1))

    def near(self):
        self.left1.wait_recv()
        self.right0.wait_recv()

    def far(self):
        self.far0.wait_recv()
        self.far1.wait_recv()


class RingSum:
    def __init__(self, cp, to, own, via, came, n):
        self.cp, self.to, self.own, self.via, self.came = cp, to, own, via, came
        self.half = (pl.ds(0, n // 2), pl.ds(n // 2, n // 2))

    def begin(self, value):
        own, half, to, cp = self.own, self.half, self.to, self.cp
        own[1] = value(2).astype(BF16)
        self.relayed = [
            cp.remote(own.at[1, half[0]], self.via.at[0], to(1)),
            cp.remote(own.at[1, half[1]], self.via.at[1], to(-1)),
        ]
        own[0] = value(1).astype(BF16)
        self.last = [cp.remote(own.at[0, half[1]], self.came.at[0, half[1]], to(1))]
        own[2] = value(3).astype(BF16)
        self.last.append(cp.remote(own.at[2, half[0]], self.came.at[1, half[0]], to(-1)))

    def relay(self):
        for i, (slot, k) in enumerate(((0, 1), (2, -1))):
            part = self.half[i]
            self.relayed[i].wait_recv()
            mine = self.own[slot, part, :].astype(F32)
            self.own[slot, part, :] = (mine + self.via[i].astype(F32)).astype(BF16)
            self.last.append(
                self.cp.remote(self.own.at[slot, part], self.came.at[i, part], self.to(k))
            )

    def finish(self):
        for c in self.last:
            c.wait_recv()


def dot(a, b):
    return jnp.dot(a, b, preferred_element_type=F32)


def distill(
    factor,
    h, d, s, w, p,
    ow, op,
    hh, dd, ss, tt, ww, pp, part, theirs, came, racc, rest,
    gx, rx, gp, own_p, via_p, came_p, own_w, via_w, came_w, sw, rh, tw, tp,
    send, recv, local,
):
    me = Place()
    cp = Copies(send, recv, local)
    sibling, across, beside = me.dev(dc=1), me.dev(dh=1), me.dev(dx=1)
    to_y, to_z = lambda k: me.dev(dy=k), lambda k: me.dev(dz=k)
    barrier(
        [to_y(k) for k in (1, 3, 2)] + [to_z(1), to_z(-1)] + [sibling, across, beside]
    )

    piece = me.z * 2 + me.core
    wide = lambda k: columns(lax.rem(me.y + k, 4), 1280)
    rows = pl.ds(pl.multiple_of(piece * 112, 16), 112)
    handed = [[], []]
    for i in (0, 1):
        for k in (2, 1, 3):
            half = columns(lax.rem(me.y + k, 4) * 2 + i, 640)
            to = dd.at[4 - k, piece, :, pl.ds(i * 640, 640)]
            handed[i].append(cp.remote(d.at[rows, half], to, to_y(k)))
    at_hidden = lambda k: columns(lax.rem(me.y + k + 4, 4), 896)
    hidden = Ring(
        cp,
        to_y,
        lambda i: h.at[pl.ds(i * 256, 256)],
        lambda k, i: hh.at[pl.ds(i * 256, 256), at_hidden(k)],
    )

    s_rows = lambda b: pl.ds(pl.multiple_of((me.core * 8 + b) * 64, 64), 64)

    def student_ring(dx):
        def place(k, i):
            return ss.at[s_rows(me.tensor(dy=k, dx=dx)), pl.ds(i * 2048, 2048)]

        own = (lambda i: place(0, i)) if dx else (lambda i: s.at[:, pl.ds(i * 2048, 2048)])
        return Ring(cp, to_y, own, place)

    student, student_beside = student_ring(0), student_ring(1)
    student_x = cp.remote(s, ss.at[s_rows(me.t)], beside)
    student_side = [cp.remote(s, ss.at[s_rows(me.t)], sibling)]

    def student_over_core(k, dx):
        block = ss.at[s_rows(me.tensor(dy=k, dx=dx))]
        student_side.append(cp.remote(block, block, sibling))

    mine, other = columns(me.core, 256), columns(1 - me.core, 256)
    weights = ((w, ww, 256), (p, pp, 320))
    at = lambda q, c, n: pl.ds(pl.multiple_of((q * 2 + c) * n, 64), n)
    pair = lambda q, n: pl.ds(pl.multiple_of(q * 2 * n, 128), 2 * n)
    swap = [
        cp.remote(a.at[:, other], b.at[at(me.q, me.core, n)], sibling) for a, b, n in weights
    ]
    own_weights = [cp.keep(a.at[:, mine], b.at[at(me.q, me.core, n)]) for a, b, n in weights]

    own_teacher = [cp.keep(h, hh.at[:, at_hidden(0)])]
    for i in range(8):
        own_teacher.append(cp.keep(d.at[pl.ds(i * 112, 112), wide(0)], dd.at[0, i]))
    own_student = cp.keep(s, ss.at[s_rows(me.t)])

    for c in own_weights:
        cp.kept_now(c)
    for c in swap:
        c.wait_recv()

    def ring(ref, n, dh):
        block = lambda k, i: ref.at[at(me.chip(dz=k, dh=dh), i, n)]
        return Ring(cp, to_z, lambda i: block(0, i), block)

    weight_rings = [ring(b, n, 0) for a, b, n in weights]
    far_rings = [ring(b, n, 1) for a, b, n in weights]
    far_weights = [
        cp.remote(b.at[pair(me.q, n)], b.at[pair(me.q, n)], across) for a, b, n in weights
    ]
    there = lambda k: lax.rem(me.z + k + 4, 4) * 2 + me.core
    over = lambda k, i: dd.at[1:4, there(k), :, pl.ds(i * 640, 640)]
    down = Ring(cp, to_z, lambda i: over(0, i), over)
    for c in handed[0]:
        c.wait_recv()
    down.start_half(0)
    hidden.start()
    for c in handed[1]:
        c.wait_recv()
    down.start_half(1)
    down_side = []

    def pass_down(k):
        block = dd.at[1:4, there(k)]
        down_side.append(cp.remote(block, block, sibling))

    pass_down(0)

    def teacher_block(out, dx, j):
        left = hh[:, columns(lax.rem(me.y + j, 4), 896)]
        for n in ((0, 256), (256, 256), (512, 128)):
            at_n = pl.ds(pl.multiple_of(lax.rem(me.xl + dx, 2) * 640 + n[0], 128), n[1])
            right = dd[j, :, :, at_n].reshape(896, n[1])
            to = slice(n[0], n[0] + n[1])
            if isinstance(j, int):
                out[:, to] = dot(left, right)
            else:
                out[:, to] += dot(left, right)

    for c in own_teacher:
        cp.kept_now(c)
    teacher_block(theirs, 1, 0)
    teacher_block(part, 0, 0)

    down.turn()
    hidden.turn()
    down.near()
    pass_down(1)
    pass_down(-1)
    down.far()
    pass_down(2)
    for r in weight_rings:
        r.start()
    student_x.wait_recv()
    student.start()
    student_beside.start()
    hidden.near()
    hidden.far()
    for c in down_side:
        c.wait_recv()

    @pl.loop(1, 4)
    def _(j):
        teacher_block(theirs, 1, j)

    chunk = lambda r: pl.ds(r * STEP, STEP)
    partial = [cp.remote(theirs.at[chunk(r)], came.at[chunk(r)], beside) for r in range(STEPS)]

    @pl.loop(1, 4)
    def _(j):
        teacher_block(part, 0, j)

    base = me.core * 512

    def t_block(r, k, dx, i=None):
        n = STEP if i is None else STEP // 2
        row = pl.multiple_of(base + r * STEP + (i or 0) * n, 16)
        return tt.at[pl.ds(row, n), columns(me.tensor(dy=k, dx=dx), 640)]

    def teacher_ring(r, dx):
        place = lambda k, i: t_block(r, k, dx, i)
        return Ring(cp, to_y, lambda i: place(0, i), place)

    rings = [[teacher_ring(r, dx) for dx in (0, 1)] for r in range(STEPS)]
    over_x = {}
    side = [[] for r in range(STEPS)]

    def over_core(r, k, dx):
        side[r].append(cp.remote(t_block(r, k, dx), t_block(r, k, dx), sibling))

    def summed(r):
        partial[r].wait_recv()
        t_block(r, 0, 0)[...] = (part[chunk(r), :] + came[chunk(r), :]).astype(BF16)
        over_x[r] = cp.remote(t_block(r, 0, 0), t_block(r, 0, 0), beside)
        rings[r][0].start()
        over_core(r, 0, 0)

    def exchanged(r):
        over_x[r].wait_recv()
        rings[r][1].start()
        over_core(r, 0, 1)

    def arrived(r):
        for dx in (0, 1):
            rings[r][dx].near()
            over_core(r, 1, dx)
            over_core(r, -1, dx)
            rings[r][dx].far()
            over_core(r, 2, dx)

    def student_output():
        for dx, r in ((0, student), (1, student_beside)):
            r.near()
            r.far()
            for k in (1, -1, 2):
                student_over_core(k, dx)
        student_over_core(0, 1)
        for r in weight_rings + far_rings:
            r.near()
            r.far()
        cp.kept_now(own_student)
        for c in student_side:
            c.wait_recv()

        @pl.loop(0, 4)
        def _(k):
            rows = pl.ds(pl.multiple_of(k * 256, 256), 256)
            racc[rows, :] = dot(ss[rows, :], ww[...])

    def residual(r):
        for c in side[r]:
            c.wait_recv()
        both = [slice(c * 512 + r * STEP, c * 512 + (r + 1) * STEP) for c in (0, 1)]
        target = dot(jnp.concatenate([tt[rows, :] for rows in both], axis=0), pp[...])
        for c, rows in enumerate(both):
            value = racc[rows, :] - target[c * STEP : (c + 1) * STEP, :]
            rest[:, rows] = value.T.astype(BF16)

    for step in range(STEPS + 3):
        if step < STEPS:
            summed(step)
        if 1 <= step <= STEPS:
            exchanged(step - 1)
            rings[step - 1][0].turn()
        if 2 <= step < STEPS + 2:
            rings[step - 2][1].turn()
        if step == 0:
            student.turn()
            student_beside.turn()
            for r in weight_rings:
                r.turn()
            for c, r in zip(far_weights, far_rings):
                c.wait_recv()
                r.start()
        if step == 2:
            for r in far_rings:
                r.turn()
        if step >= 3:
            arrived(step - 3)
        if step == STEPS:
            student_output()
        if step > STEPS:
            residual(step - STEPS - 1)
    for r in range(2, STEPS):
        residual(r)

    def project(**to):
        return dot(rest[...], tt[:, columns(me.chip(**to), 640)])

    def weigh(**to):
        return dot(rest[...], ss[:, columns(me.chip(**to), 512)])

    from_x = {}
    for k in (2, 1, 3, 0):
        gx[k] = weigh(dz=k, dh=1).astype(BF16)
        from_x[k] = cp.remote(gx.at[k], rx.at[k], across)
    far_sum, near_sum = [
        RingSum(cp, to_z, own_p.at[i], via_p.at[i], came_p.at[i], 256) for i in (0, 1)
    ]
    weight_sum = RingSum(cp, to_z, own_w, via_w, came_w, 256)
    far_sum.begin(lambda k: project(dz=k, dh=1))
    near_sum.begin(lambda k: project(dz=k))

    def crossed(k):
        value = weigh(dz=k)
        from_x[k].wait_recv()
        return value + rx[k].astype(F32)

    far_sum.relay()
    weight_sum.begin(crossed)
    near_sum.relay()
    gp[...] = project(dh=1)
    far_sum.finish()
    sw[...] = (
        gp[...] + came_p[0, 0].astype(F32) + came_p[0, 1].astype(F32)
    ).astype(BF16)
    back = cp.remote(sw, rh, across)
    weight_sum.relay()
    last = []

    def hand_out(staged, out, n, parts):
        for i in range(n // 64):
            block = slice(i * 128, i * 128 + 128)
            value = gp[:, block]
            for r in parts:
                value += r[:, block].astype(F32)
            staged[block, :] = (value * factor).T
        theirs = pl.ds(pl.multiple_of((1 - me.core) * n, 64), n)
        ours = pl.ds(pl.multiple_of(me.core * n, 64), n)
        last.append(cp.remote(staged.at[theirs], out.at[:, mine], sibling))
        cp.keep(staged.at[ours], out.at[:, mine])

    gp[:, :512] = weigh()
    from_x[0].wait_recv()
    weight_sum.finish()
    hand_out(tw, ow, 256, [rx.at[0], came_w.at[0], came_w.at[1]])
    gp[...] = project()
    near_sum.finish()
    back.wait_recv()
    hand_out(tp, op, 320, [came_p.at[1, 0], came_p.at[1, 1], rh])
    for c in last:
        c.wait_recv()
    cp.drain()


def on_device(*args):
    narrow = lambda *shape: pltpu.VMEM(shape, BF16)
    wide = lambda *shape: pltpu.VMEM(shape, F32)
    return tuple(
        pl.pallas_call(
            functools.partial(distill, 1.0 / math.sqrt(8192)),
            out_shape=[
                jax.ShapeDtypeStruct((256, 512), F32),
                jax.ShapeDtypeStruct((320, 512), F32),
            ],
            in_specs=[pl.BlockSpec(memory_space=pl.ANY)] * 5,
            out_specs=[pl.BlockSpec(memory_space=pltpu.VMEM)] * 2,
            scratch_shapes=[
                narrow(512, 3584),
                narrow(4, 8, 112, 1280),
                narrow(1024, 4096),
                narrow(1024, 5120),
                narrow(4096, 256),
                narrow(5120, 256),
                wide(512, 640),
                wide(512, 640),
                wide(512, 640),
                wide(1024, 256),
                narrow(256, 1024),
                narrow(4, 256, 512),
                narrow(4, 256, 512),
                wide(256, 640),
                narrow(2, 3, 256, 640),
                narrow(2, 2, 128, 640),
                narrow(2, 2, 256, 640),
                narrow(3, 256, 512),
                narrow(2, 128, 512),
                narrow(2, 256, 512),
                narrow(256, 640),
                narrow(256, 640),
                wide(512, 256),
                wide(640, 256),
                pltpu.SemaphoreType.DMA((COPIES,)),
                pltpu.SemaphoreType.DMA((COPIES,)),
                pltpu.SemaphoreType.DMA((16,)),
            ],
            compiler_params=pltpu.CompilerParams(
                collective_id=1, has_side_effects=True, vmem_limit_bytes=VMEM_MIB * 2**20
            ),
        )(*args)
    )


def solution(mesh):
    in_specs = (
        P("dp", "tensor"),
        P("tensor", None),
        P(("dp", "tensor"), None),
        P("dp", "tensor"),
        P("dp", "tensor"),
    )
    out_specs = (P("dp", "tensor"), P("dp", "tensor"))

    return jax.shard_map(
        on_device, mesh=mesh, in_specs=in_specs, out_specs=out_specs, check_vma=False
    )
```

```python
import functools
import math

import jax
import jax.numpy as jnp
from jax import lax
from jax.experimental import pallas as pl
from jax.experimental.pallas import tpu as pltpu
from jax.sharding import PartitionSpec as P

MESH = pl.DeviceIdType.MESH
BF16 = jnp.bfloat16
F32 = jnp.float32
COPIES = 208
STEPS = 4
VMEM_MIB = 56
STEP = 512 // STEPS


class Place:
    def __init__(self):
        self.d = lax.axis_index("dp")
        self.t = lax.axis_index("tensor")
        self.core = lax.rem(self.d, 2)
        self.q = lax.div(self.d, 2)
        self.z = lax.rem(self.q, 4)
        self.xh = lax.div(self.q, 4)
        self.y = lax.div(self.t, 2)
        self.xl = lax.rem(self.t, 2)

    def dev(self, dy=0, dx=0, dz=0, dh=0, dc=0):
        d = self.dp(dz, dh, dc)
        return (d, self.tensor(dy, dx))

    def tensor(self, dy=0, dx=0):
        return lax.rem(self.y + dy + 4, 4) * 2 + lax.rem(self.xl + dx, 2)

    def chip(self, dz=0, dh=0):
        return lax.rem(self.xh + dh, 2) * 4 + lax.rem(self.z + dz + 4, 4)

    def dp(self, dz=0, dh=0, dc=0):
        return self.chip(dz, dh) * 2 + lax.rem(self.core + dc, 2)


class Copies:
    def __init__(self, send, recv, local):
        self.send, self.recv, self.local = send, recv, local
        self.n = 0
        self.m = 0
        self.sent = []
        self.kept = []

    def remote(self, src, dst, to):
        c = pltpu.make_async_remote_copy(
            src_ref=src,
            dst_ref=dst,
            send_sem=self.send.at[self.n],
            recv_sem=self.recv.at[self.n],
            device_id=to,
            device_id_type=MESH,
        )
        self.n += 1
        c.start()
        self.sent.append(c)
        return c

    def keep(self, src, dst):
        c = pltpu.make_async_copy(src, dst, self.local.at[self.m])
        self.m += 1
        c.start()
        self.kept.append(c)
        return c

    def kept_now(self, c):
        c.wait()
        self.kept = [k for k in self.kept if k is not c]

    def drain(self):
        for c in self.kept:
            c.wait()
        for c in self.sent:
            c.wait_send()


def barrier(devices):
    sem = pltpu.get_barrier_semaphore()
    for dev in devices:
        pl.semaphore_signal(sem, inc=1, device_id=dev, device_id_type=MESH)
    pl.semaphore_wait(sem, len(devices))


def columns(index, width):
    return pl.ds(pl.multiple_of(index * width, 128), width)


class Ring:
    def __init__(self, cp, to, own, place):
        self.cp, self.to, self.own, self.place = cp, to, own, place

    def start(self):
        send = lambda h, k: self.cp.remote(self.own(h), self.place(0, h), self.to(k))
        self.left0, self.right1 = send(0, 1), send(1, -1)
        self.left1, self.right0 = send(1, 1), send(0, -1)

    def start_half(self, h):
        send = lambda k: self.cp.remote(self.own(h), self.place(0, h), self.to(k))
        if h == 0:
            self.left0, self.right0 = send(1), send(-1)
        else:
            self.right1, self.left1 = send(-1), send(1)

    def turn(self):
        self.left0.wait_recv()
        self.far0 = self.cp.remote(self.place(-1, 0), self.place(-1, 0), self.to(1))
        self.right1.wait_recv()
        self.far1 = self.cp.remote(self.place(1, 1), self.place(1, 1), self.to(-1))

    def near(self):
        self.left1.wait_recv()
        self.right0.wait_recv()

    def far(self):
        self.far0.wait_recv()
        self.far1.wait_recv()


class RingSum:
    def __init__(self, cp, to, own, via, came, n):
        self.cp, self.to, self.own, self.via, self.came = cp, to, own, via, came
        self.half = (pl.ds(0, n // 2), pl.ds(n // 2, n // 2))

    def begin(self, value):
        own, half, to, cp = self.own, self.half, self.to, self.cp
        own[1] = value(2).astype(BF16)
        self.relayed = [
            cp.remote(own.at[1, half[0]], self.via.at[0], to(1)),
            cp.remote(own.at[1, half[1]], self.via.at[1], to(-1)),
        ]
        own[0] = value(1).astype(BF16)
        self.last = [cp.remote(own.at[0, half[1]], self.came.at[0, half[1]], to(1))]
        own[2] = value(3).astype(BF16)
        self.last.append(cp.remote(own.at[2, half[0]], self.came.at[1, half[0]], to(-1)))

    def relay(self):
        for i, (slot, k) in enumerate(((0, 1), (2, -1))):
            part = self.half[i]
            self.relayed[i].wait_recv()
            mine = self.own[slot, part, :].astype(F32)
            self.own[slot, part, :] = (mine + self.via[i].astype(F32)).astype(BF16)
            self.last.append(
                self.cp.remote(self.own.at[slot, part], self.came.at[i, part], self.to(k))
            )

    def finish(self):
        for c in self.last:
            c.wait_recv()


def dot(a, b):
    return jnp.dot(a, b, preferred_element_type=F32)


def distill(
    factor,
    h, d, s, w, p,
    ow, op,
    hh, dd, ss, tt, ww, pp, part, theirs, came, racc, rest,
    gx, rx, gp, own_p, via_p, came_p, own_w, via_w, came_w, sw, rh, tw, tp,
    send, recv, local,
):
    me = Place()
    cp = Copies(send, recv, local)
    sibling, across, beside = me.dev(dc=1), me.dev(dh=1), me.dev(dx=1)
    to_y, to_z = lambda k: me.dev(dy=k), lambda k: me.dev(dz=k)
    barrier(
        [to_y(k) for k in (1, 3, 2)] + [to_z(1), to_z(-1)] + [sibling, across, beside]
    )

    piece = me.z * 2 + me.core
    wide = lambda k: columns(lax.rem(me.y + k, 4), 1280)
    rows = pl.ds(pl.multiple_of(piece * 112, 16), 112)
    handed = [[], []]
    for i in (0, 1):
        for k in (2, 1, 3):
            half = columns(lax.rem(me.y + k, 4) * 2 + i, 640)
            to = dd.at[4 - k, piece, :, pl.ds(i * 640, 640)]
            handed[i].append(cp.remote(d.at[rows, half], to, to_y(k)))
    at_hidden = lambda k: columns(lax.rem(me.y + k + 4, 4), 896)
    hidden = Ring(
        cp,
        to_y,
        lambda i: h.at[pl.ds(i * 256, 256)],
        lambda k, i: hh.at[pl.ds(i * 256, 256), at_hidden(k)],
    )

    s_rows = lambda b: pl.ds(pl.multiple_of((me.core * 8 + b) * 64, 64), 64)

    def student_ring(dx):
        def place(k, i):
            return ss.at[s_rows(me.tensor(dy=k, dx=dx)), pl.ds(i * 2048, 2048)]

        own = (lambda i: place(0, i)) if dx else (lambda i: s.at[:, pl.ds(i * 2048, 2048)])
        return Ring(cp, to_y, own, place)

    student, student_beside = student_ring(0), student_ring(1)
    student_x = cp.remote(s, ss.at[s_rows(me.t)], beside)
    student_side = [cp.remote(s, ss.at[s_rows(me.t)], sibling)]

    def student_over_core(k, dx):
        block = ss.at[s_rows(me.tensor(dy=k, dx=dx))]
        student_side.append(cp.remote(block, block, sibling))

    mine, other = columns(me.core, 256), columns(1 - me.core, 256)
    weights = ((w, ww, 256), (p, pp, 320))
    at = lambda q, c, n: pl.ds(pl.multiple_of((q * 2 + c) * n, 64), n)
    pair = lambda q, n: pl.ds(pl.multiple_of(q * 2 * n, 128), 2 * n)
    swap = [
        cp.remote(a.at[:, other], b.at[at(me.q, me.core, n)], sibling) for a, b, n in weights
    ]
    own_weights = [cp.keep(a.at[:, mine], b.at[at(me.q, me.core, n)]) for a, b, n in weights]

    own_teacher = [cp.keep(h, hh.at[:, at_hidden(0)])]
    for i in range(8):
        own_teacher.append(cp.keep(d.at[pl.ds(i * 112, 112), wide(0)], dd.at[0, i]))
    own_student = cp.keep(s, ss.at[s_rows(me.t)])

    for c in own_weights:
        cp.kept_now(c)
    for c in swap:
        c.wait_recv()

    def ring(ref, n, dh):
        block = lambda k, i: ref.at[at(me.chip(dz=k, dh=dh), i, n)]
        return Ring(cp, to_z, lambda i: block(0, i), block)

    weight_rings = [ring(b, n, 0) for a, b, n in weights]
    far_rings = [ring(b, n, 1) for a, b, n in weights]
    far_weights = [
        cp.remote(b.at[pair(me.q, n)], b.at[pair(me.q, n)], across) for a, b, n in weights
    ]
    there = lambda k: lax.rem(me.z + k + 4, 4) * 2 + me.core
    over = lambda k, i: dd.at[1:4, there(k), :, pl.ds(i * 640, 640)]
    down = Ring(cp, to_z, lambda i: over(0, i), over)
    for c in handed[0]:
        c.wait_recv()
    down.start_half(0)
    hidden.start()
    for c in handed[1]:
        c.wait_recv()
    down.start_half(1)
    down_side = []

    def pass_down(k):
        block = dd.at[1:4, there(k)]
        down_side.append(cp.remote(block, block, sibling))

    pass_down(0)

    def teacher_block(out, dx, j):
        left = hh[:, columns(lax.rem(me.y + j, 4), 896)]
        for n in ((0, 256), (256, 256), (512, 128)):
            at_n = pl.ds(pl.multiple_of(lax.rem(me.xl + dx, 2) * 640 + n[0], 128), n[1])
            right = dd[j, :, :, at_n].reshape(896, n[1])
            to = slice(n[0], n[0] + n[1])
            if isinstance(j, int):
                out[:, to] = dot(left, right)
            else:
                out[:, to] += dot(left, right)

    for c in own_teacher:
        cp.kept_now(c)
    teacher_block(theirs, 1, 0)
    teacher_block(part, 0, 0)

    down.turn()
    hidden.turn()
    down.near()
    pass_down(1)
    pass_down(-1)
    down.far()
    pass_down(2)
    for r in weight_rings:
        r.start()
    student_x.wait_recv()
    student.start()
    student_beside.start()
    hidden.near()
    hidden.far()
    for c in down_side:
        c.wait_recv()

    @pl.loop(1, 4)
    def _(j):
        teacher_block(theirs, 1, j)

    chunk = lambda r: pl.ds(r * STEP, STEP)
    partial = [cp.remote(theirs.at[chunk(r)], came.at[chunk(r)], beside) for r in range(STEPS)]

    @pl.loop(1, 4)
    def _(j):
        teacher_block(part, 0, j)

    base = me.core * 512

    def t_block(r, k, dx, i=None):
        n = STEP if i is None else STEP // 2
        row = pl.multiple_of(base + r * STEP + (i or 0) * n, 16)
        return tt.at[pl.ds(row, n), columns(me.tensor(dy=k, dx=dx), 640)]

    def teacher_ring(r, dx):
        place = lambda k, i: t_block(r, k, dx, i)
        return Ring(cp, to_y, lambda i: place(0, i), place)

    rings = [[teacher_ring(r, dx) for dx in (0, 1)] for r in range(STEPS)]
    over_x = {}
    side = [[] for r in range(STEPS)]

    def over_core(r, k, dx):
        side[r].append(cp.remote(t_block(r, k, dx), t_block(r, k, dx), sibling))

    def summed(r):
        partial[r].wait_recv()
        t_block(r, 0, 0)[...] = (part[chunk(r), :] + came[chunk(r), :]).astype(BF16)
        over_x[r] = cp.remote(t_block(r, 0, 0), t_block(r, 0, 0), beside)
        rings[r][0].start()
        over_core(r, 0, 0)

    def exchanged(r):
        over_x[r].wait_recv()
        rings[r][1].start()
        over_core(r, 0, 1)

    def arrived(r):
        for dx in (0, 1):
            rings[r][dx].near()
            over_core(r, 1, dx)
            over_core(r, -1, dx)
            rings[r][dx].far()
            over_core(r, 2, dx)

    def student_output():
        for dx, r in ((0, student), (1, student_beside)):
            r.near()
            r.far()
            for k in (1, -1, 2):
                student_over_core(k, dx)
        student_over_core(0, 1)
        for r in weight_rings + far_rings:
            r.near()
            r.far()
        cp.kept_now(own_student)
        for c in student_side:
            c.wait_recv()

        @pl.loop(0, 4)
        def _(k):
            rows = pl.ds(pl.multiple_of(k * 256, 256), 256)
            racc[rows, :] = dot(ss[rows, :], ww[...])

    def residual(r):
        for c in side[r]:
            c.wait_recv()
        both = [slice(c * 512 + r * STEP, c * 512 + (r + 1) * STEP) for c in (0, 1)]
        target = dot(jnp.concatenate([tt[rows, :] for rows in both], axis=0), pp[...])
        for c, rows in enumerate(both):
            value = racc[rows, :] - target[c * STEP : (c + 1) * STEP, :]
            rest[:, rows] = value.T.astype(BF16)

    for step in range(STEPS + 3):
        if step < STEPS:
            summed(step)
        if 1 <= step <= STEPS:
            exchanged(step - 1)
            rings[step - 1][0].turn()
        if 2 <= step < STEPS + 2:
            rings[step - 2][1].turn()
        if step == 0:
            student.turn()
            student_beside.turn()
            for r in weight_rings:
                r.turn()
            for c, r in zip(far_weights, far_rings):
                c.wait_recv()
                r.start()
        if step == 2:
            for r in far_rings:
                r.turn()
        if step >= 3:
            arrived(step - 3)
        if step == STEPS - 1:
            student_output()
        if step > STEPS:
            residual(step - STEPS - 1)
    for r in range(2, STEPS):
        residual(r)

    def project(**to):
        return dot(rest[...], tt[:, columns(me.chip(**to), 640)])

    def weigh(**to):
        return dot(rest[...], ss[:, columns(me.chip(**to), 512)])

    from_x = {}
    for k in (2, 1, 3, 0):
        gx[k] = weigh(dz=k, dh=1).astype(BF16)
        from_x[k] = cp.remote(gx.at[k], rx.at[k], across)
    far_sum, near_sum = [
        RingSum(cp, to_z, own_p.at[i], via_p.at[i], came_p.at[i], 256) for i in (0, 1)
    ]
    weight_sum = RingSum(cp, to_z, own_w, via_w, came_w, 256)
    far_sum.begin(lambda k: project(dz=k, dh=1))
    near_sum.begin(lambda k: project(dz=k))

    def crossed(k):
        value = weigh(dz=k)
        from_x[k].wait_recv()
        return value + rx[k].astype(F32)

    far_sum.relay()
    weight_sum.begin(crossed)
    near_sum.relay()
    gp[...] = project(dh=1)
    far_sum.finish()
    sw[...] = (
        gp[...] + came_p[0, 0].astype(F32) + came_p[0, 1].astype(F32)
    ).astype(BF16)
    back = cp.remote(sw, rh, across)
    weight_sum.relay()
    last = []

    def hand_out(staged, out, n, parts):
        for i in range(n // 64):
            block = slice(i * 128, i * 128 + 128)
            value = gp[:, block]
            for r in parts:
                value += r[:, block].astype(F32)
            staged[block, :] = (value * factor).T
        theirs = pl.ds(pl.multiple_of((1 - me.core) * n, 64), n)
        ours = pl.ds(pl.multiple_of(me.core * n, 64), n)
        last.append(cp.remote(staged.at[theirs], out.at[:, mine], sibling))
        cp.keep(staged.at[ours], out.at[:, mine])

    gp[:, :512] = weigh()
    from_x[0].wait_recv()
    weight_sum.finish()
    hand_out(tw, ow, 256, [rx.at[0], came_w.at[0], came_w.at[1]])
    gp[...] = project()
    near_sum.finish()
    back.wait_recv()
    hand_out(tp, op, 320, [came_p.at[1, 0], came_p.at[1, 1], rh])
    for c in last:
        c.wait_recv()
    cp.drain()


def hand_over(gw, gp, ow, op):
    ow[...] = gw[...]
    op[...] = gp[...]


def on_device(*args):
    narrow = lambda *shape: pltpu.VMEM(shape, BF16)
    wide = lambda *shape: pltpu.VMEM(shape, F32)
    shapes = [jax.ShapeDtypeStruct((rows, 512), F32) for rows in (256, 320)]
    grads = pl.pallas_call(
            functools.partial(distill, 1.0 / math.sqrt(8192)),
            out_shape=shapes,
            in_specs=[pl.BlockSpec(memory_space=pl.ANY)] * 5,
            out_specs=[pl.BlockSpec(memory_space=pl.ANY)] * 2,
            scratch_shapes=[
                narrow(512, 3584),
                narrow(4, 8, 112, 1280),
                narrow(1024, 4096),
                narrow(1024, 5120),
                narrow(4096, 256),
                narrow(5120, 256),
                wide(512, 640),
                wide(512, 640),
                wide(512, 640),
                wide(1024, 256),
                narrow(256, 1024),
                narrow(4, 256, 512),
                narrow(4, 256, 512),
                wide(256, 640),
                narrow(2, 3, 256, 640),
                narrow(2, 2, 128, 640),
                narrow(2, 2, 256, 640),
                narrow(3, 256, 512),
                narrow(2, 128, 512),
                narrow(2, 256, 512),
                narrow(256, 640),
                narrow(256, 640),
                wide(512, 256),
                wide(640, 256),
                pltpu.SemaphoreType.DMA((COPIES,)),
                pltpu.SemaphoreType.DMA((COPIES,)),
                pltpu.SemaphoreType.DMA((16,)),
            ],
            compiler_params=pltpu.CompilerParams(
                collective_id=1, has_side_effects=True, vmem_limit_bytes=VMEM_MIB * 2**20
            ),
    )(*args)
    return tuple(
        pl.pallas_call(
            hand_over,
            out_shape=shapes,
            in_specs=[pl.BlockSpec(memory_space=pltpu.VMEM)] * 2,
            out_specs=[pl.BlockSpec(memory_space=pltpu.VMEM)] * 2,
        )(*grads)
    )


def solution(mesh):
    in_specs = (
        P("dp", "tensor"),
        P("tensor", None),
        P(("dp", "tensor"), None),
        P("dp", "tensor"),
        P("dp", "tensor"),
    )
    out_specs = (P("dp", "tensor"), P("dp", "tensor"))

    return jax.shard_map(
        on_device, mesh=mesh, in_specs=in_specs, out_specs=out_specs, check_vma=False
    )
```

```python
import functools
import math

import jax
import jax.numpy as jnp
from jax import lax
from jax.experimental import pallas as pl
from jax.experimental.pallas import tpu as pltpu
from jax.sharding import PartitionSpec as P

MESH = pl.DeviceIdType.MESH
BF16 = jnp.bfloat16
F32 = jnp.float32
COPIES = 208
STEPS = 4
VMEM_MIB = 56
STEP = 512 // STEPS


class Place:
    def __init__(self):
        self.d = lax.axis_index("dp")
        self.t = lax.axis_index("tensor")
        self.core = lax.rem(self.d, 2)
        self.q = lax.div(self.d, 2)
        self.z = lax.rem(self.q, 4)
        self.xh = lax.div(self.q, 4)
        self.y = lax.div(self.t, 2)
        self.xl = lax.rem(self.t, 2)

    def dev(self, dy=0, dx=0, dz=0, dh=0, dc=0):
        d = self.dp(dz, dh, dc)
        return (d, self.tensor(dy, dx))

    def tensor(self, dy=0, dx=0):
        return lax.rem(self.y + dy + 4, 4) * 2 + lax.rem(self.xl + dx, 2)

    def chip(self, dz=0, dh=0):
        return lax.rem(self.xh + dh, 2) * 4 + lax.rem(self.z + dz + 4, 4)

    def dp(self, dz=0, dh=0, dc=0):
        return self.chip(dz, dh) * 2 + lax.rem(self.core + dc, 2)


class Copies:
    def __init__(self, send, recv, local):
        self.send, self.recv, self.local = send, recv, local
        self.n = 0
        self.m = 0
        self.sent = []
        self.kept = []

    def remote(self, src, dst, to):
        c = pltpu.make_async_remote_copy(
            src_ref=src,
            dst_ref=dst,
            send_sem=self.send.at[self.n],
            recv_sem=self.recv.at[self.n],
            device_id=to,
            device_id_type=MESH,
        )
        self.n += 1
        c.start()
        self.sent.append(c)
        return c

    def keep(self, src, dst):
        c = pltpu.make_async_copy(src, dst, self.local.at[self.m])
        self.m += 1
        c.start()
        self.kept.append(c)
        return c

    def kept_now(self, c):
        c.wait()
        self.kept = [k for k in self.kept if k is not c]

    def drain(self):
        for c in self.kept:
            c.wait()
        for c in self.sent:
            c.wait_send()


def barrier(devices):
    sem = pltpu.get_barrier_semaphore()
    for dev in devices:
        pl.semaphore_signal(sem, inc=1, device_id=dev, device_id_type=MESH)
    pl.semaphore_wait(sem, len(devices))


def columns(index, width):
    return pl.ds(pl.multiple_of(index * width, 128), width)


class Ring:
    def __init__(self, cp, to, own, place):
        self.cp, self.to, self.own, self.place = cp, to, own, place

    def start(self):
        send = lambda h, k: self.cp.remote(self.own(h), self.place(0, h), self.to(k))
        self.left0, self.right1 = send(0, 1), send(1, -1)
        self.left1, self.right0 = send(1, 1), send(0, -1)

    def start_half(self, h):
        send = lambda k: self.cp.remote(self.own(h), self.place(0, h), self.to(k))
        if h == 0:
            self.left0, self.right0 = send(1), send(-1)
        else:
            self.right1, self.left1 = send(-1), send(1)

    def turn(self):
        self.left0.wait_recv()
        self.far0 = self.cp.remote(self.place(-1, 0), self.place(-1, 0), self.to(1))
        self.right1.wait_recv()
        self.far1 = self.cp.remote(self.place(1, 1), self.place(1, 1), self.to(-1))

    def near(self):
        self.left1.wait_recv()
        self.right0.wait_recv()

    def far(self):
        self.far0.wait_recv()
        self.far1.wait_recv()


class RingSum:
    def __init__(self, cp, to, own, via, came, n):
        self.cp, self.to, self.own, self.via, self.came = cp, to, own, via, came
        self.half = (pl.ds(0, n // 2), pl.ds(n // 2, n // 2))

    def begin(self, value):
        own, half, to, cp = self.own, self.half, self.to, self.cp
        own[1] = value(2).astype(BF16)
        self.relayed = [
            cp.remote(own.at[1, half[0]], self.via.at[0], to(1)),
            cp.remote(own.at[1, half[1]], self.via.at[1], to(-1)),
        ]
        own[0] = value(1).astype(BF16)
        self.last = [cp.remote(own.at[0, half[1]], self.came.at[0, half[1]], to(1))]
        own[2] = value(3).astype(BF16)
        self.last.append(cp.remote(own.at[2, half[0]], self.came.at[1, half[0]], to(-1)))

    def relay(self):
        for i, (slot, k) in enumerate(((0, 1), (2, -1))):
            part = self.half[i]
            self.relayed[i].wait_recv()
            mine = self.own[slot, part, :].astype(F32)
            self.own[slot, part, :] = (mine + self.via[i].astype(F32)).astype(BF16)
            self.last.append(
                self.cp.remote(self.own.at[slot, part], self.came.at[i, part], self.to(k))
            )

    def finish(self):
        for c in self.last:
            c.wait_recv()


def dot(a, b):
    return jnp.dot(a, b, preferred_element_type=F32)


def distill(
    factor,
    h, d, s, w, p,
    ow, op,
    hh, dd, ss, tt, ww, pp, part, theirs, came, racc, rest,
    gx, rx, gp, own_p, via_p, came_p, own_w, via_w, came_w, sw, rh, tw, tp,
    send, recv, local,
):
    me = Place()
    cp = Copies(send, recv, local)
    sibling, across, beside = me.dev(dc=1), me.dev(dh=1), me.dev(dx=1)
    to_y, to_z = lambda k: me.dev(dy=k), lambda k: me.dev(dz=k)
    barrier(
        [to_y(k) for k in (1, 3, 2)] + [to_z(1), to_z(-1)] + [sibling, across, beside]
    )

    piece = me.z * 2 + me.core
    wide = lambda k: columns(lax.rem(me.y + k, 4), 1280)
    rows = pl.ds(pl.multiple_of(piece * 112, 16), 112)
    handed = [[], []]
    for i in (0, 1):
        for k in (2, 1, 3):
            half = columns(lax.rem(me.y + k, 4) * 2 + i, 640)
            to = dd.at[4 - k, piece, :, pl.ds(i * 640, 640)]
            handed[i].append(cp.remote(d.at[rows, half], to, to_y(k)))
    at_hidden = lambda k: columns(lax.rem(me.y + k + 4, 4), 896)
    hidden = Ring(
        cp,
        to_y,
        lambda i: h.at[pl.ds(i * 256, 256)],
        lambda k, i: hh.at[pl.ds(i * 256, 256), at_hidden(k)],
    )

    s_rows = lambda b: pl.ds(pl.multiple_of((me.core * 8 + b) * 64, 64), 64)

    def student_ring(dx):
        def place(k, i):
            return ss.at[s_rows(me.tensor(dy=k, dx=dx)), pl.ds(i * 2048, 2048)]

        own = (lambda i: place(0, i)) if dx else (lambda i: s.at[:, pl.ds(i * 2048, 2048)])
        return Ring(cp, to_y, own, place)

    student, student_beside = student_ring(0), student_ring(1)
    student_x = cp.remote(s, ss.at[s_rows(me.t)], beside)
    student_side = [cp.remote(s, ss.at[s_rows(me.t)], sibling)]

    def student_over_core(k, dx):
        block = ss.at[s_rows(me.tensor(dy=k, dx=dx))]
        student_side.append(cp.remote(block, block, sibling))

    mine, other = columns(me.core, 256), columns(1 - me.core, 256)
    weights = ((w, ww, 256), (p, pp, 320))
    at = lambda q, c, n: pl.ds(pl.multiple_of((q * 2 + c) * n, 64), n)
    pair = lambda q, n: pl.ds(pl.multiple_of(q * 2 * n, 128), 2 * n)
    swap = [
        cp.remote(a.at[:, other], b.at[at(me.q, me.core, n)], sibling) for a, b, n in weights
    ]
    own_weights = [cp.keep(a.at[:, mine], b.at[at(me.q, me.core, n)]) for a, b, n in weights]

    own_teacher = [cp.keep(h, hh.at[:, at_hidden(0)])]
    for i in range(8):
        own_teacher.append(cp.keep(d.at[pl.ds(i * 112, 112), wide(0)], dd.at[0, i]))
    own_student = cp.keep(s, ss.at[s_rows(me.t)])

    for c in own_weights:
        cp.kept_now(c)
    for c in swap:
        c.wait_recv()

    def ring(ref, n, dh):
        block = lambda k, i: ref.at[at(me.chip(dz=k, dh=dh), i, n)]
        return Ring(cp, to_z, lambda i: block(0, i), block)

    weight_rings = [ring(b, n, 0) for a, b, n in weights]
    far_rings = [ring(b, n, 1) for a, b, n in weights]
    far_weights = [
        cp.remote(b.at[pair(me.q, n)], b.at[pair(me.q, n)], across) for a, b, n in weights
    ]
    there = lambda k: lax.rem(me.z + k + 4, 4) * 2 + me.core
    over = lambda k, i: dd.at[1:4, there(k), :, pl.ds(i * 640, 640)]
    down = Ring(cp, to_z, lambda i: over(0, i), over)
    for c in handed[0]:
        c.wait_recv()
    down.start_half(0)
    hidden.start()
    for c in handed[1]:
        c.wait_recv()
    down.start_half(1)
    down_side = []

    def pass_down(k):
        block = dd.at[1:4, there(k)]
        down_side.append(cp.remote(block, block, sibling))

    pass_down(0)

    def teacher_block(out, dx, j):
        left = hh[:, columns(lax.rem(me.y + j, 4), 896)]
        for n in ((0, 256), (256, 256), (512, 128)):
            at_n = pl.ds(pl.multiple_of(lax.rem(me.xl + dx, 2) * 640 + n[0], 128), n[1])
            right = dd[j, :, :, at_n].reshape(896, n[1])
            to = slice(n[0], n[0] + n[1])
            if isinstance(j, int):
                out[:, to] = dot(left, right)
            else:
                out[:, to] += dot(left, right)

    for c in own_teacher:
        cp.kept_now(c)
    teacher_block(theirs, 1, 0)
    teacher_block(part, 0, 0)

    down.turn()
    hidden.turn()
    down.near()
    pass_down(1)
    pass_down(-1)
    down.far()
    pass_down(2)
    for r in weight_rings:
        r.start()
    student_x.wait_recv()
    student.start()
    student_beside.start()
    hidden.near()
    hidden.far()
    for c in down_side:
        c.wait_recv()

    @pl.loop(1, 4)
    def _(j):
        teacher_block(theirs, 1, j)

    chunk = lambda r: pl.ds(r * STEP, STEP)
    partial = [cp.remote(theirs.at[chunk(r)], came.at[chunk(r)], beside) for r in range(STEPS)]

    @pl.loop(1, 4)
    def _(j):
        teacher_block(part, 0, j)

    base = me.core * 512

    def t_block(r, k, dx, i=None):
        n = STEP if i is None else STEP // 2
        row = pl.multiple_of(base + r * STEP + (i or 0) * n, 16)
        return tt.at[pl.ds(row, n), columns(me.tensor(dy=k, dx=dx), 640)]

    def teacher_ring(r, dx):
        place = lambda k, i: t_block(r, k, dx, i)
        return Ring(cp, to_y, lambda i: place(0, i), place)

    rings = [[teacher_ring(r, dx) for dx in (0, 1)] for r in range(STEPS)]
    over_x = {}
    side = [[] for r in range(STEPS)]

    def over_core(r, k, dx):
        side[r].append(cp.remote(t_block(r, k, dx), t_block(r, k, dx), sibling))

    def summed(r):
        partial[r].wait_recv()
        t_block(r, 0, 0)[...] = (part[chunk(r), :] + came[chunk(r), :]).astype(BF16)
        over_x[r] = cp.remote(t_block(r, 0, 0), t_block(r, 0, 0), beside)
        rings[r][0].start()
        over_core(r, 0, 0)

    def exchanged(r):
        over_x[r].wait_recv()
        rings[r][1].start()
        over_core(r, 0, 1)

    def arrived(r):
        for dx in (0, 1):
            rings[r][dx].near()
            over_core(r, 1, dx)
            over_core(r, -1, dx)
            rings[r][dx].far()
            over_core(r, 2, dx)

    def student_output():
        for dx, r in ((0, student), (1, student_beside)):
            r.near()
            r.far()
            for k in (1, -1, 2):
                student_over_core(k, dx)
        student_over_core(0, 1)
        for r in weight_rings + far_rings:
            r.near()
            r.far()
        cp.kept_now(own_student)
        for c in student_side:
            c.wait_recv()

        @pl.loop(0, 4)
        def _(k):
            rows = pl.ds(pl.multiple_of(k * 256, 256), 256)
            racc[rows, :] = dot(ss[rows, :], ww[...])

    def residual(r):
        for c in side[r]:
            c.wait_recv()
        both = [slice(c * 512 + r * STEP, c * 512 + (r + 1) * STEP) for c in (0, 1)]
        target = dot(jnp.concatenate([tt[rows, :] for rows in both], axis=0), pp[...])
        for c, rows in enumerate(both):
            value = racc[rows, :] - target[c * STEP : (c + 1) * STEP, :]
            rest[:, rows] = value.T.astype(BF16)

    for step in range(STEPS + 3):
        if step < STEPS:
            summed(step)
        if 1 <= step <= STEPS:
            exchanged(step - 1)
            rings[step - 1][0].turn()
        if 2 <= step < STEPS + 2:
            rings[step - 2][1].turn()
        if step == 0:
            student.turn()
            student_beside.turn()
            for r in weight_rings:
                r.turn()
            for c, r in zip(far_weights, far_rings):
                c.wait_recv()
                r.start()
        if step == 2:
            for r in far_rings:
                r.turn()
        if step >= 3:
            arrived(step - 3)
        if step == STEPS - 2:
            student_output()
        if step > STEPS:
            residual(step - STEPS - 1)
    for r in range(2, STEPS):
        residual(r)

    def project(**to):
        return dot(rest[...], tt[:, columns(me.chip(**to), 640)])

    def weigh(**to):
        return dot(rest[...], ss[:, columns(me.chip(**to), 512)])

    from_x = {}

    def cross(k):
        gx[k] = weigh(dz=k, dh=1).astype(BF16)
        from_x[k] = cp.remote(gx.at[k], rx.at[k], across)

    cross(2)
    far_sum, near_sum = [
        RingSum(cp, to_z, own_p.at[i], via_p.at[i], came_p.at[i], 256) for i in (0, 1)
    ]
    weight_sum = RingSum(cp, to_z, own_w, via_w, came_w, 256)
    far_sum.begin(lambda k: project(dz=k, dh=1))
    for k in (1, 3, 0):
        cross(k)
    near_sum.begin(lambda k: project(dz=k))

    def crossed(k):
        value = weigh(dz=k)
        from_x[k].wait_recv()
        return value + rx[k].astype(F32)

    far_sum.relay()
    weight_sum.begin(crossed)
    near_sum.relay()
    gp[...] = project(dh=1)
    far_sum.finish()
    sw[...] = (
        gp[...] + came_p[0, 0].astype(F32) + came_p[0, 1].astype(F32)
    ).astype(BF16)
    back = cp.remote(sw, rh, across)
    weight_sum.relay()
    last = []

    def hand_out(staged, out, n, parts):
        for i in range(n // 64):
            block = slice(i * 128, i * 128 + 128)
            value = gp[:, block]
            for r in parts:
                value += r[:, block].astype(F32)
            staged[block, :] = (value * factor).T
        theirs = pl.ds(pl.multiple_of((1 - me.core) * n, 64), n)
        ours = pl.ds(pl.multiple_of(me.core * n, 64), n)
        last.append(cp.remote(staged.at[theirs], out.at[:, mine], sibling))
        cp.keep(staged.at[ours], out.at[:, mine])

    gp[:, :512] = weigh()
    from_x[0].wait_recv()
    weight_sum.finish()
    hand_out(tw, ow, 256, [rx.at[0], came_w.at[0], came_w.at[1]])
    gp[...] = project()
    near_sum.finish()
    back.wait_recv()
    hand_out(tp, op, 320, [came_p.at[1, 0], came_p.at[1, 1], rh])
    for c in last:
        c.wait_recv()
    cp.drain()


def hand_over(gw, gp, ow, op):
    ow[...] = gw[...]
    op[...] = gp[...]


def on_device(*args):
    narrow = lambda *shape: pltpu.VMEM(shape, BF16)
    wide = lambda *shape: pltpu.VMEM(shape, F32)
    shapes = [jax.ShapeDtypeStruct((rows, 512), F32) for rows in (256, 320)]
    grads = pl.pallas_call(
            functools.partial(distill, 1.0 / math.sqrt(8192)),
            out_shape=shapes,
            in_specs=[pl.BlockSpec(memory_space=pl.ANY)] * 5,
            out_specs=[pl.BlockSpec(memory_space=pl.ANY)] * 2,
            scratch_shapes=[
                narrow(512, 3584),
                narrow(4, 8, 112, 1280),
                narrow(1024, 4096),
                narrow(1024, 5120),
                narrow(4096, 256),
                narrow(5120, 256),
                wide(512, 640),
                wide(512, 640),
                wide(512, 640),
                wide(1024, 256),
                narrow(256, 1024),
                narrow(4, 256, 512),
                narrow(4, 256, 512),
                wide(256, 640),
                narrow(2, 3, 256, 640),
                narrow(2, 2, 128, 640),
                narrow(2, 2, 256, 640),
                narrow(3, 256, 512),
                narrow(2, 128, 512),
                narrow(2, 256, 512),
                narrow(256, 640),
                narrow(256, 640),
                wide(512, 256),
                wide(640, 256),
                pltpu.SemaphoreType.DMA((COPIES,)),
                pltpu.SemaphoreType.DMA((COPIES,)),
                pltpu.SemaphoreType.DMA((16,)),
            ],
            compiler_params=pltpu.CompilerParams(
                collective_id=1, has_side_effects=True, vmem_limit_bytes=VMEM_MIB * 2**20
            ),
    )(*args)
    return tuple(
        pl.pallas_call(
            hand_over,
            out_shape=shapes,
            in_specs=[pl.BlockSpec(memory_space=pltpu.VMEM)] * 2,
            out_specs=[pl.BlockSpec(memory_space=pltpu.VMEM)] * 2,
        )(*grads)
    )


def solution(mesh):
    in_specs = (
        P("dp", "tensor"),
        P("tensor", None),
        P(("dp", "tensor"), None),
        P("dp", "tensor"),
        P("dp", "tensor"),
    )
    out_specs = (P("dp", "tensor"), P("dp", "tensor"))

    return jax.shard_map(
        on_device, mesh=mesh, in_specs=in_specs, out_specs=out_specs, check_vma=False
    )
```
